512 devices in a mesh: member: 8 (over z), space: 64 (over y, x, core).
Axes of the slice: x: 4, y: 8, z: 8, core: 2. Of those that a mesh axis runs over, the one named last changes fastest.
Arguments:
- ensemble: float32 [512, 256, 1024], P('member', 'space'), may hold values from -6 to 6
- speed_row: float32 [256, 1024], P('space'), may hold values from -0.3 to 0.3
- speed_col: float32 [256, 1024], P('space'), may hold values from -0.3 to 0.3
- obs_cell: int32 [64, 8, 1, 2, 128], P('space', 'member'), may hold values from 0 to 511
- obs_value: float32 [64, 8, 1, 2, 128], P('space', 'member'), may hold values from -6 to 6
- obs_var: float32 [64, 8, 1, 2, 128], P('space', 'member'), may hold values from 0.5 to 4
- obs_count: int32 [64, 8, 1, 2], P('space', 'member'), may hold values from 0 to 128
- loc_slots: int32 [64, 8, 1, 12], P('space', 'member'), may hold values from 0 to 17, as said below
Outputs:
- analysis_ensemble: float32 [512, 256, 1024], P('member', 'space')
The draws below stay inside these ranges and needn't reach their ends.
Inputs may be any that keep to these rules, and one draw needn't show every extreme that they name: `loc_slots`: each patch and cycle lists 12 different neighbour slots. `obs_cell`: a cell of the tile's own patch, counted row by row. `obs_count`: the live observations of a tile are its first ones.
All inputs are finite; a program needn't handle non-finite values.
Results may differ from the reference program's by a relative error of at most 0.0003.
Values sent between devices are 32-bit elements; how exact they have to be, the bound alone decides.
No kernel may reach another device: no remote copies, remote signals or barrier semaphores. Data moves between devices by JAX's collectives and lax.ppermute only.
A program may use at most 64 MiB of HBM per device.

```python
import math
import jax
import jax.numpy as jnp
from jax import lax

M = 512
PCOLS = 128
ROWS_DEV = 4
OBS = 128
TPR = 2
LOCN = 12
ASTEPS = 2
CYCLES = 1
NC = 1024
NR = 256
PATCH = 512
GRID_PR = 64
GRID_PC = 8


def wave_field(key, member_coef, amplitude, mode_count):
    wave_key = jax.random.fold_in(key, 21)
    row_freq = jax.random.uniform(jax.random.fold_in(wave_key, 1), (mode_count,), minval=-1.0, maxval=1.0)
    col_freq = jax.random.uniform(jax.random.fold_in(wave_key, 2), (mode_count,), minval=0.02, maxval=1.0)
    phase_shift = jax.random.uniform(jax.random.fold_in(wave_key, 3), (mode_count,), minval=0.0, maxval=2.0 * math.pi)
    row_index = jnp.arange(NR, dtype=jnp.float32)
    col_index = jnp.arange(NC, dtype=jnp.float32)
    wave_angle = row_freq[:, None, None] * row_index[None, :, None] + col_freq[:, None, None] * col_index[None, None, :] + phase_shift[:, None, None]
    wave_basis = jnp.concatenate([jnp.cos(wave_angle), jnp.sin(wave_angle)], axis=0)
    wave_basis = wave_basis * jnp.concatenate([amplitude, amplitude])[:, None, None]
    smooth = jnp.dot(member_coef, wave_basis.reshape(2 * mode_count, NR * NC), precision=lax.Precision.HIGHEST)
    return smooth.reshape(M, NR, NC)


def draw_ensemble(key, part):
    key = jax.random.fold_in(key, 11)
    mode_count = 40
    coef_key = jax.random.fold_in(key, 5)
    rough_key = jax.random.fold_in(key, 7)
    steps_along = jnp.arange(mode_count, dtype=jnp.float32) / (mode_count - 1.0)
    amplitude = 0.03 ** steps_along
    member_coef = jax.random.normal(coef_key, (M, 2 * mode_count))
    rough_part = jax.random.normal(rough_key, (M, NR, NC))
    smooth = wave_field(key, member_coef.astype(jnp.float32), amplitude.astype(jnp.float32), mode_count)
    return jnp.clip(smooth + rough_part.astype(jnp.float32), -6.0, 6.0).astype(jnp.float32)


def draw_loc_slots(key, part):
    total = GRID_PR * GRID_PC * CYCLES
    keys_all = jax.random.split(key, total)
    orders = jax.vmap(lambda one_key: jax.random.permutation(one_key, 9 * TPR))(keys_all)
    return orders[:, :LOCN].reshape(GRID_PR, GRID_PC, CYCLES, LOCN).astype(jnp.int32)


def set_ends(drawn, rng, low, top_value):
    spot = [jax.random.randint(jax.random.fold_in(rng, axis), (), 0, length) for axis, length in enumerate(drawn.shape)]
    main_axis = drawn.shape.index(max(drawn.shape))
    beside = spot[:main_axis] + [(spot[main_axis] + 1) % drawn.shape[main_axis]] + spot[main_axis + 1:]
    return drawn.at[tuple(spot)].set(low).at[tuple(beside)].set(top_value)


def steps_of(key, shape, pieces, least, high):
    level = 1.0
    for dim, blocks in pieces:
        draws = jax.random.uniform(jax.random.fold_in(jax.random.fold_in(key, 6), dim), (blocks,), jnp.float32, least / len(pieces), high / len(pieces))
        level = level * jnp.repeat(jnp.exp(draws), shape[dim] // blocks).reshape((-1,) + (1,) * (len(shape) - 1 - dim))
    return level


def bell_draw(rng, dims, deviation, bound, cuts=(), held_as=jnp.bfloat16):
    array = deviation * jax.random.normal(rng, dims, jnp.float32)
    if cuts:
        array = array * steps_of(rng, dims, cuts, -0.22, 0.18)
    return jnp.clip(array, -bound, bound).astype(held_as)


def setup_inputs(seed: int = 0) -> dict:
    streams_of = jax.random.split(jax.random.key(seed), 9)
    return {
        "ensemble": draw_ensemble(jax.random.fold_in(streams_of[8], 71), 0),
        "speed_row": jnp.clip(jax.random.uniform(streams_of[1], (NR, NC), jnp.float32, -0.3, 0.3) * steps_of(streams_of[1], (NR, NC), ((0, 64),), -0.4, 0.0), -0.3, 0.3),
        "speed_col": jnp.clip(jax.random.uniform(streams_of[2], (NR, NC), jnp.float32, -0.3, 0.3) * steps_of(streams_of[2], (NR, NC), ((0, 64),), -0.4, 0.0), -0.3, 0.3),
        "obs_cell": set_ends(jax.random.randint(streams_of[3], (GRID_PR, GRID_PC, CYCLES, TPR, OBS), 0, PATCH), jax.random.fold_in(streams_of[3], 1), 0, PATCH - 1).astype(jnp.int32),
        "obs_value": bell_draw(streams_of[4], (GRID_PR, GRID_PC, CYCLES, TPR, OBS), 1.0, 6.0, ((0, 64), (1, 8)), jnp.float32),
        "obs_var": jnp.clip(jnp.exp(math.log(4.0) - 2.0794415 * jax.random.uniform(streams_of[5], (GRID_PR, GRID_PC, CYCLES, TPR, OBS), jnp.float32) ** steps_of(streams_of[5], (GRID_PR, GRID_PC, CYCLES, TPR, OBS), ((0, 64), (1, 8)), -0.2, 0.2)), 0.5, 4.0),
        "obs_count": set_ends(jax.random.randint(streams_of[6], (GRID_PR, GRID_PC, CYCLES, TPR), 0, OBS + 1), jax.random.fold_in(streams_of[6], 1), 0, OBS).astype(jnp.int32),
        "loc_slots": draw_loc_slots(jax.random.fold_in(streams_of[8], 71), 0),
    }


diffusion = 0.2

def blend(centre, above_row, below_row, left_col, right_col, speed_rows, speed_cols):
    return (1.0 - 4.0 * diffusion) * centre + (diffusion + 0.5 * speed_rows) * above_row + (diffusion - 0.5 * speed_rows) * below_row + (diffusion + 0.5 * speed_cols) * left_col + (diffusion - 0.5 * speed_cols) * right_col

def member_split(flat_patch):
    centre_mean = jnp.mean(flat_patch, axis=0)
    return (centre_mean, flat_patch - centre_mean[None, :])

def tile_terms(centre_mean, anomaly, cell_index, values, variance, counts):
    flat_cells = cell_index.reshape(-1)
    members = anomaly.shape[0]
    tile_y = jnp.take(anomaly, flat_cells, axis=1).reshape(members, cell_index.shape[0], cell_index.shape[1]).transpose(1, 0, 2)
    innovation = values - jnp.take(centre_mean, flat_cells).reshape(cell_index.shape)
    live_mask = lax.broadcasted_iota(jnp.int32, cell_index.shape, 1) < counts[:, None]
    weight = jnp.where(live_mask, 1.0 / variance, jnp.zeros_like(variance))
    return (tile_y, innovation, weight)

def taper_of(slot_list, per_patch):
    offsets = slot_list // per_patch
    row_off = offsets // 3 - 1
    col_off = offsets % 3 - 1
    return 1.0 / (1.0 + (row_off * row_off + col_off * col_off).astype(jnp.float32))

def assimilate(centre_mean, anomaly, chosen_y, chosen_innov, chosen_weight, taper_vec):
    members = anomaly.shape[0]
    scaled = taper_vec[:, None] * chosen_weight / (members - 1.0)
    gram_matrix = jnp.einsum('lmo,lno->mn', chosen_y * scaled[:, None, :], chosen_y, precision=lax.Precision.HIGHEST)
    drive_vec = jnp.einsum('lmo,lo->m', chosen_y, scaled * chosen_innov, precision=lax.Precision.HIGHEST)
    unit_matrix = jnp.eye(members, dtype=jnp.float32)
    factor_low = jnp.linalg.cholesky(unit_matrix + gram_matrix)
    forward = jax.scipy.linalg.solve_triangular(factor_low, unit_matrix, lower=True)
    inverse = jnp.dot(forward.T, forward, precision=lax.Precision.HIGHEST)
    mean_shift = jnp.dot(inverse, drive_vec, precision=lax.Precision.HIGHEST)
    mean_new = centre_mean + jnp.dot(mean_shift, anomaly, precision=lax.Precision.HIGHEST)
    spread = 0.5 * (anomaly + jnp.dot(inverse, anomaly, precision=lax.Precision.HIGHEST))
    return mean_new[None, :] + spread

def reference(ensemble, speed_row, speed_col, obs_cell, obs_value, obs_var, obs_count, loc_slots):

    def advect_one(grid_field):
        return blend(grid_field, jnp.roll(grid_field, 1, 0), jnp.roll(grid_field, -1, 0), jnp.roll(grid_field, 1, 1), jnp.roll(grid_field, -1, 1), speed_row, speed_col)
    grid_state = ensemble
    patch_count = GRID_PR * GRID_PC
    for cycle_index in range(CYCLES):
        for step_index in range(ASTEPS):
            grid_state = lax.map(advect_one, grid_state)
        patches = grid_state.reshape(M, GRID_PR, ROWS_DEV, GRID_PC, PCOLS).transpose(1, 3, 0, 2, 4).reshape(patch_count, M, PATCH)

        def make_tiles(packed):
            flat_patch, cell_index, values, variance, counts = packed
            centre_mean, anomaly = member_split(flat_patch)
            return tile_terms(centre_mean, anomaly, cell_index, values, variance, counts)
        all_y, all_innov, all_weight = lax.map(make_tiles, (patches, obs_cell[:, :, cycle_index].reshape(patch_count, TPR, OBS), obs_value[:, :, cycle_index].reshape(patch_count, TPR, OBS), obs_var[:, :, cycle_index].reshape(patch_count, TPR, OBS), obs_count[:, :, cycle_index].reshape(patch_count, TPR)))
        all_y = all_y.reshape(GRID_PR, GRID_PC, TPR, M, OBS)
        all_innov = all_innov.reshape(GRID_PR, GRID_PC, TPR, OBS)
        all_weight = all_weight.reshape(GRID_PR, GRID_PC, TPR, OBS)

        def update_one(packed):
            flat_patch, patch_number, slot_list = packed
            patch_row = patch_number // GRID_PC
            patch_col = patch_number % GRID_PC
            offsets = slot_list // TPR
            within = slot_list % TPR
            source_row = (patch_row + offsets // 3 - 1) % GRID_PR
            source_col = (patch_col + offsets % 3 - 1) % GRID_PC
            chosen_y = all_y[source_row, source_col, within]
            chosen_innov = all_innov[source_row, source_col, within]
            chosen_weight = all_weight[source_row, source_col, within]
            centre_mean, anomaly = member_split(flat_patch)
            return assimilate(centre_mean, anomaly, chosen_y, chosen_innov, chosen_weight, taper_of(slot_list, TPR))
        updated = lax.map(update_one, (patches, jnp.arange(patch_count, dtype=jnp.int32), loc_slots[:, :, cycle_index].reshape(patch_count, LOCN)))
        grid_state = updated.reshape(GRID_PR, GRID_PC, M, ROWS_DEV, PCOLS).transpose(2, 0, 3, 1, 4).reshape(M, NR, NC)
    return grid_state
```

```python
import functools

import jax
import jax.numpy as jnp
from jax import lax
from jax.experimental import pallas as pl
from jax.experimental.pallas import tpu as pltpu
from jax.sharding import PartitionSpec as P

K = 0.2
HI = lax.Precision.HIGHEST
SUB = 8
NT = (((1,), (1,)), ((), ()))


def split3(x):
    a = x.astype(jnp.bfloat16)
    rest = x - a.astype(jnp.float32)
    b = rest.astype(jnp.bfloat16)
    c = (rest - b.astype(jnp.float32)).astype(jnp.bfloat16)
    return a, b, c


def eye(n):
    rows = lax.broadcasted_iota(jnp.int32, (n, n), 0)
    cols = lax.broadcasted_iota(jnp.int32, (n, n), 1)
    return jnp.where(rows == cols, 1.0, 0.0).astype(jnp.float32)


def advect_kernel(planes, before, after, speed_row, speed_col, out, coef):
    rows, members, width = planes.shape
    blocks = out.shape[0]
    cols = out.shape[3]
    groups = members // SUB
    top, bottom = before[2 * groups], after[2 * groups]
    for r in range(rows + 2):
        if r == 0:
            u, v = top[0:1], top[1:2]
        elif r == rows + 1:
            u, v = bottom[0:1], bottom[1:2]
        else:
            u, v = speed_row[r - 1 : r], speed_col[r - 1 : r]
        for n, c in enumerate((K + 0.5 * u, K - 0.5 * u, K + 0.5 * v, K - 0.5 * v)):
            coef[r, n] = jnp.broadcast_to(c, (SUB, width))

    def step(field, first):
        new = []
        for n in range(1, len(field) - 1):
            r = first + n - 1
            x = field[n]
            new.append(
                (1.0 - 4.0 * K) * x
                + coef[r, 0] * field[n - 1]
                + coef[r, 1] * field[n + 1]
                + coef[r, 2] * pltpu.roll(x, 1, 1)
                + coef[r, 3] * pltpu.roll(x, width - 1, 1)
            )
        return new

    def body(g, carry):
        at = pl.ds(pl.multiple_of(g * SUB, SUB), SUB)
        field = [before[g], before[groups + g]]
        field += [planes[i, at, :] for i in range(rows)]
        field += [after[g], after[groups + g]]
        field = step(step(field, 0), 1)
        for i in range(rows):
            for b in range(blocks):
                out[b, i, at, :] = field[i][:, b * cols : (b + 1) * cols]
        return carry

    lax.fori_loop(0, groups, body, 0)


def patch_matrix(state):
    parts, rows, members, cols = state.shape
    return jnp.concatenate(
        [state[:, i].reshape(parts * members, cols) for i in range(rows)], axis=1
    )


def tile_kernel(count, state, cell, value, variance, tiles, centre):
    parts, rows, members, cols = state.shape
    total = parts * members
    cells = rows * cols
    per_patch, obs = cell.shape
    x = patch_matrix(state)
    mean = jnp.sum(x, axis=0, keepdims=True) * (1.0 / total)
    for i in range(rows):
        centre[i : i + 1, :] = mean[:, i * cols : (i + 1) * cols]
    anomaly = jnp.concatenate([x - mean, jnp.broadcast_to(mean, (SUB, cells))], axis=0)
    parts3 = split3(anomaly)
    row = lax.broadcasted_iota(jnp.int32, (cells, obs), 0)
    lane = lax.broadcasted_iota(jnp.int32, (1, obs), 1)
    below = lax.broadcasted_iota(jnp.int32, (SUB, obs), 0)
    for t in range(per_patch):
        pick = jnp.where(row == cell[t : t + 1, :], 1.0, 0.0).astype(jnp.bfloat16)
        y = sum(jnp.dot(p, pick, preferred_element_type=jnp.float32) for p in parts3[::-1])
        live = lane < count[t]
        weight = jnp.where(live, 1.0 / variance[t : t + 1, :], 0.0)
        scale = jnp.sqrt(weight * (1.0 / (total - 1.0)))
        tiles[t, 0:total, :] = y[:total] * scale
        innovation = (value[t : t + 1, :] - y[total:]) * scale
        tiles[t, total : total + SUB, :] = jnp.where(below == 0, innovation, 0.0)


def spd_inverse(s):
    n = s.shape[0]
    unit = eye(n)
    size = jnp.sum(s * s)
    bound = jnp.minimum(jnp.sqrt(size), jnp.max(jnp.sum(jnp.abs(s), axis=0)))
    bound = jnp.maximum(bound, 1.0) * 1.0001
    scale = 2.0 / (1.0 + bound)
    x = scale * unit
    e = unit - scale * s
    rho = (bound - 1.0) / (bound + 1.0)

    def more(carry):
        return carry[2] > 1e-3

    def square(carry):
        x, e, rho = carry
        both = jnp.dot(jnp.concatenate([x, e], axis=0), e, precision=HI)
        square_rho = rho * rho
        scale = 2.0 / (2.0 - square_rho)
        x = scale * (x + both[:n])
        e = scale * both[n:] + (1.0 - scale) * unit
        return x, e, square_rho / (2.0 - square_rho)

    x, e, rho = lax.while_loop(more, square, (x, e, rho))
    for _ in range(2):
        e = unit - jnp.dot(s, x, precision=HI)
        x = x + jnp.dot(x, e, precision=HI)
    return x


def update_kernel(per_patch, slots, state, centre, *refs):
    near = refs[:9]
    out, z, inv = refs[9:]
    parts, rows, members, cols = state.shape
    total = parts * members
    half = total // 2
    mask = jnp.int32(0)
    for n in range(slots.shape[0]):
        mask = mask | lax.shift_left(jnp.int32(1), slots[n])
    place = jnp.int32(0)
    for q in range(9 * per_patch):
        o, t = q // per_patch, q % per_patch
        r, s = o // 3 - 1, o % 3 - 1
        taper = 1.0 / (1.0 + r * r + s * s)
        chosen = lax.shift_right_logical(mask, q) & 1

        @pl.when(chosen == 1)
        def _():
            obs = near[o].shape[2]
            z[:, pl.ds(pl.multiple_of(place * obs, obs), obs)] = near[o][t] * (taper**0.5)

        place = place + chosen
    gram = lax.dot_general(z[...], z[0:total, :], NT, precision=HI)
    drive = gram[total : total + SUB]
    s11 = gram[:half, :half] + eye(half)
    s12 = gram[:half, half:]
    s22 = gram[half:total, half:] + eye(half)
    inv11 = spd_inverse(s11)
    w = jnp.dot(inv11, s12, precision=HI)
    schur = s22 - lax.dot_general(s12, w, (((0,), (0,)), ((), ())), precision=HI)
    inv22 = spd_inverse(0.5 * (schur + schur.T))
    low = jnp.dot(w, inv22, precision=HI)
    inv[0:half, 0:half] = inv11 + lax.dot_general(low, w, NT, precision=HI)
    inv[0:half, half:] = -low
    inv[half:, 0:half] = -low.T
    inv[half:, half:] = inv22
    shift = jnp.dot(drive, inv[...], precision=HI)[0:1]
    mean = jnp.concatenate([centre[i : i + 1, :] for i in range(rows)], axis=1)
    anomaly = patch_matrix(state) - mean
    result = jnp.dot(0.5 * inv[...] + shift, anomaly, precision=HI)
    result = result + (mean + 0.5 * anomaly)
    for p in range(parts):
        for i in range(rows):
            out[p, i] = result[p * members : (p + 1) * members, i * cols : (i + 1) * cols]


VMEM = pl.BlockSpec(memory_space=pltpu.VMEM)
SMEM = pl.BlockSpec(memory_space=pltpu.SMEM)
PARAMS = pltpu.CompilerParams(vmem_limit_bytes=48 * 1024 * 1024)


def f32(*shape):
    return jax.ShapeDtypeStruct(shape, jnp.float32)


def shifted(x, axis, by):
    n = lax.axis_size(axis)
    return lax.ppermute(x, axis, [(i, (i + by) % n) for i in range(n)])


def swap(x):
    return lax.all_to_all(x, "member", split_axis=0, concat_axis=0, tiled=True)


def on_device(ensemble, speed_row, speed_col, obs_cell, obs_value, obs_var, obs_count, loc_slots):
    members, rows, width = ensemble.shape
    parts = lax.axis_size("member")
    cols = width // parts
    groups = members // SUB
    per_patch, obs = obs_cell.shape[3:]
    total = parts * members

    planes = ensemble.transpose(1, 0, 2)

    def edge(first, row):
        speeds = jnp.concatenate(
            [speed_row[row : row + 1], speed_col[row : row + 1], jnp.zeros((SUB - 2, width), jnp.float32)]
        )
        body = planes[first : first + 2].reshape(2 * groups, SUB, width)
        return jnp.concatenate([body, speeds[None]])

    before = shifted(edge(rows - 2, rows - 1), "space", 1)
    after = shifted(edge(0, 0), "space", -1)
    state = pl.pallas_call(
        advect_kernel,
        out_shape=f32(parts, rows, members, cols),
        in_specs=[VMEM] * 5,
        out_specs=VMEM,
        scratch_shapes=[pltpu.VMEM((rows + 2, 4, SUB, width), jnp.float32)],
        compiler_params=PARAMS,
        name="advect",
    )(planes, before, after, speed_row, speed_col)
    state = swap(state)
    tiles, centre = pl.pallas_call(
        tile_kernel,
        out_shape=(f32(per_patch, total + SUB, obs), f32(rows, cols)),
        in_specs=[SMEM] + [VMEM] * 4,
        out_specs=(VMEM, VMEM),
        compiler_params=PARAMS,
        name="tiles",
    )(obs_count[0, 0, 0], state, obs_cell[0, 0, 0], obs_value[0, 0, 0], obs_var[0, 0, 0])
    left = shifted(tiles, "member", 1)
    right = shifted(tiles, "member", -1)
    line = (left, tiles, right)
    near = [shifted(x, "space", 1) for x in line] + list(line) + [shifted(x, "space", -1) for x in line]
    slots = loc_slots[0, 0, 0]
    state = pl.pallas_call(
        functools.partial(update_kernel, per_patch),
        out_shape=f32(parts, rows, members, cols),
        in_specs=[SMEM] + [VMEM] * 11,
        out_specs=VMEM,
        scratch_shapes=[
            pltpu.VMEM((total + SUB, slots.shape[0] * obs), jnp.float32),
            pltpu.VMEM((total, total), jnp.float32),
        ],
        compiler_params=PARAMS,
        name="update",
    )(slots, state, centre, *near)
    state = swap(state)
    return state.transpose(2, 1, 0, 3).reshape(members, rows, width)


def solution(mesh):
    return jax.shard_map(
        on_device,
        mesh=mesh,
        in_specs=(
            P("member", "space", None),
            P("space", None),
            P("space", None),
            P("space", "member", None, None, None),
            P("space", "member", None, None, None),
            P("space", "member", None, None, None),
            P("space", "member", None, None),
            P("space", "member", None, None),
        ),
        out_specs=P("member", "space", None),
        check_vma=False,
    )
```

```python
import functools

import jax
import jax.numpy as jnp
from jax import lax
from jax.experimental import pallas as pl
from jax.experimental.pallas import tpu as pltpu
from jax.sharding import PartitionSpec as P

K = 0.2
HI = lax.Precision.HIGHEST
SUB = 8
NT = (((1,), (1,)), ((), ()))


def split3(x):
    a = x.astype(jnp.bfloat16)
    rest = x - a.astype(jnp.float32)
    b = rest.astype(jnp.bfloat16)
    c = (rest - b.astype(jnp.float32)).astype(jnp.bfloat16)
    return a, b, c


def eye(n):
    rows = lax.broadcasted_iota(jnp.int32, (n, n), 0)
    cols = lax.broadcasted_iota(jnp.int32, (n, n), 1)
    return jnp.where(rows == cols, 1.0, 0.0).astype(jnp.float32)


def parity(axis):
    return lax.rem(lax.axis_index(axis), 2)


def edge_kernel(ensemble, speed_row, speed_col, across, within):
    members, rows, width = ensemble.shape
    groups = members // SUB
    odd = parity("space") == 1

    def put(at, low, high):
        across[at] = jnp.where(odd, high, low)
        within[at] = jnp.where(odd, low, high)

    for g in range(groups):
        for n in range(2):
            low = ensemble[g * SUB : (g + 1) * SUB, n, :]
            high = ensemble[g * SUB : (g + 1) * SUB, rows - 2 + n, :]
            put(n * groups + g, low, high)
    across[2 * groups] = jnp.zeros((SUB, width), jnp.float32)
    within[2 * groups] = jnp.zeros((SUB, width), jnp.float32)
    for n, speed in enumerate((speed_row, speed_col)):
        put((2 * groups, slice(n, n + 1)), speed[0:1], speed[rows - 1 : rows])


def advect_kernel(planes, across, within, speed_row, speed_col, out, coef):
    rows, members, width = planes.shape
    blocks = out.shape[0]
    cols = out.shape[3]
    groups = members // SUB
    odd = parity("space") == 1

    def before(at):
        return jnp.where(odd, within[at], across[at])

    def after(at):
        return jnp.where(odd, across[at], within[at])

    top, bottom = before(2 * groups), after(2 * groups)
    for r in range(rows + 2):
        if r == 0:
            u, v = top[0:1], top[1:2]
        elif r == rows + 1:
            u, v = bottom[0:1], bottom[1:2]
        else:
            u, v = speed_row[r - 1 : r], speed_col[r - 1 : r]
        for n, c in enumerate((K + 0.5 * u, K - 0.5 * u, K + 0.5 * v, K - 0.5 * v)):
            coef[r, n] = jnp.broadcast_to(c, (SUB, width))

    def step(field, first):
        new = []
        for n in range(1, len(field) - 1):
            r = first + n - 1
            x = field[n]
            new.append(
                (1.0 - 4.0 * K) * x
                + coef[r, 0] * field[n - 1]
                + coef[r, 1] * field[n + 1]
                + coef[r, 2] * pltpu.roll(x, 1, 1)
                + coef[r, 3] * pltpu.roll(x, width - 1, 1)
            )
        return new

    def body(g, carry):
        at = pl.ds(pl.multiple_of(g * SUB, SUB), SUB)
        field = [before(g), before(groups + g)]
        field += [planes[i, at, :] for i in range(rows)]
        field += [after(g), after(groups + g)]
        field = step(step(field, 0), 1)
        for i in range(rows):
            for b in range(blocks):
                out[b, i, at, :] = field[i][:, b * cols : (b + 1) * cols]
        return carry

    lax.fori_loop(0, groups, body, 0)


def patch_matrix(state):
    parts, rows, members, cols = state.shape
    return jnp.concatenate(
        [state[:, i].reshape(parts * members, cols) for i in range(rows)], axis=1
    )


def tile_kernel(count, state, cell, value, variance, tiles, centre):
    parts, rows, members, cols = state.shape
    total = parts * members
    cells = rows * cols
    per_patch, obs = cell.shape
    x = patch_matrix(state)
    mean = jnp.sum(x, axis=0, keepdims=True) * (1.0 / total)
    for i in range(rows):
        centre[i : i + 1, :] = mean[:, i * cols : (i + 1) * cols]
    anomaly = jnp.concatenate([x - mean, jnp.broadcast_to(mean, (SUB, cells))], axis=0)
    parts3 = split3(anomaly)
    row = lax.broadcasted_iota(jnp.int32, (cells, obs), 0)
    lane = lax.broadcasted_iota(jnp.int32, (1, obs), 1)
    below = lax.broadcasted_iota(jnp.int32, (SUB, obs), 0)
    for t in range(per_patch):
        pick = jnp.where(row == cell[t : t + 1, :], 1.0, 0.0).astype(jnp.bfloat16)
        y = sum(jnp.dot(p, pick, preferred_element_type=jnp.float32) for p in parts3[::-1])
        live = lane < count[t]
        weight = jnp.where(live, 1.0 / variance[t : t + 1, :], 0.0)
        scale = jnp.sqrt(weight * (1.0 / (total - 1.0)))
        tiles[t, 0:total, :] = y[:total] * scale
        innovation = (value[t : t + 1, :] - y[total:]) * scale
        tiles[t, total : total + SUB, :] = jnp.where(below == 0, innovation, 0.0)


def spd_inverse(s):
    n = s.shape[0]
    unit = eye(n)
    size = jnp.sum(s * s)
    bound = jnp.minimum(jnp.sqrt(size), jnp.max(jnp.sum(jnp.abs(s), axis=0)))
    bound = jnp.maximum(bound, 1.0) * 1.0001
    scale = 2.0 / (1.0 + bound)
    x = scale * unit
    e = unit - scale * s
    rho = (bound - 1.0) / (bound + 1.0)

    def more(carry):
        return carry[2] > 1e-3

    def square(carry):
        x, e, rho = carry
        both = jnp.dot(jnp.concatenate([x, e], axis=0), e, precision=HI)
        square_rho = rho * rho
        scale = 2.0 / (2.0 - square_rho)
        x = scale * (x + both[:n])
        e = scale * both[n:] + (1.0 - scale) * unit
        return x, e, square_rho / (2.0 - square_rho)

    x, e, rho = lax.while_loop(more, square, (x, e, rho))
    for _ in range(2):
        e = unit - jnp.dot(s, x, precision=HI)
        x = x + jnp.dot(x, e, precision=HI)
    return x


def update_kernel(per_patch, slots, state, centre, lines, corners, out, z, inv):
    parts, rows, members, cols = state.shape
    total = parts * members
    half = total // 2
    odd_row, odd_col = parity("space"), parity("member")
    mask = jnp.int32(0)
    for n in range(slots.shape[0]):
        o, t = lax.div(slots[n], per_patch), lax.rem(slots[n], per_patch)
        r, s = lax.div(o, 3), lax.rem(o, 3)
        r = r + odd_row * (2 - 2 * r)
        s = s + odd_col * (2 - 2 * s)
        mask = mask | lax.shift_left(jnp.int32(1), (r * 3 + s) * per_patch + t)
    place = jnp.int32(0)
    for q in range(9 * per_patch):
        o, t = q // per_patch, q % per_patch
        r, s = o // 3 - 1, o % 3 - 1
        taper = 1.0 / (1.0 + r * r + s * s)
        chosen = lax.shift_right_logical(mask, q) & 1
        ref = corners[r, s][0] if r and s else lines[r, s]
        row = t + (corners[r, s][1] if r and s else 0)

        @pl.when(chosen == 1)
        def _():
            obs = ref.shape[2]
            z[:, pl.ds(pl.multiple_of(place * obs, obs), obs)] = ref[row] * (taper**0.5)

        place = place + chosen
    gram = lax.dot_general(z[...], z[0:total, :], NT, precision=HI)
    drive = gram[total : total + SUB]
    s11 = gram[:half, :half] + eye(half)
    s12 = gram[:half, half:]
    s22 = gram[half:total, half:] + eye(half)
    inv11 = spd_inverse(s11)
    w = jnp.dot(inv11, s12, precision=HI)
    schur = s22 - lax.dot_general(s12, w, (((0,), (0,)), ((), ())), precision=HI)
    inv22 = spd_inverse(0.5 * (schur + schur.T))
    low = jnp.dot(w, inv22, precision=HI)
    inv[0:half, 0:half] = inv11 + lax.dot_general(low, w, NT, precision=HI)
    inv[0:half, half:] = -low
    inv[half:, 0:half] = -low.T
    inv[half:, half:] = inv22
    shift = jnp.dot(drive, inv[...], precision=HI)[0:1]
    mean = jnp.concatenate([centre[i : i + 1, :] for i in range(rows)], axis=1)
    anomaly = patch_matrix(state) - mean
    result = jnp.dot(0.5 * inv[...] + shift, anomaly, precision=HI)
    result = result + (mean + 0.5 * anomaly)
    for p in range(parts):
        for i in range(rows):
            out[p, i] = result[p * members : (p + 1) * members, i * cols : (i + 1) * cols]


def update(per_patch, slots, state, centre, own, odd_z, even_z, across, within, within_c, across_c, *rest):
    lines = {(0, 0): own, (0, 1): even_z, (0, -1): odd_z, (-1, 0): across, (1, 0): within}
    corners = {
        (-1, 1): (across_c, 0),
        (-1, -1): (across_c, per_patch),
        (1, 1): (within_c, 0),
        (1, -1): (within_c, per_patch),
    }
    update_kernel(per_patch, slots, state, centre, lines, corners, *rest)


VMEM = pl.BlockSpec(memory_space=pltpu.VMEM)
SMEM = pl.BlockSpec(memory_space=pltpu.SMEM)
PARAMS = pltpu.CompilerParams(vmem_limit_bytes=28 * 1024 * 1024)


def f32(*shape):
    return jax.ShapeDtypeStruct(shape, jnp.float32)


def paired(x, axis, first):
    n = lax.axis_size(axis)
    pairs = [(i, (i + 1) % n) for i in range(first, n, 2)]
    return lax.ppermute(x, axis, pairs + [(j, i) for i, j in pairs])


def swap(x):
    return lax.all_to_all(x, "member", split_axis=0, concat_axis=0, tiled=True)


def on_device(ensemble, speed_row, speed_col, obs_cell, obs_value, obs_var, obs_count, loc_slots):
    members, rows, width = ensemble.shape
    parts = lax.axis_size("member")
    cols = width // parts
    groups = members // SUB
    per_patch, obs = obs_cell.shape[3:]
    total = parts * members

    planes = ensemble.transpose(1, 0, 2)
    across, within = pl.pallas_call(
        edge_kernel,
        out_shape=(f32(2 * groups + 1, SUB, width), f32(2 * groups + 1, SUB, width)),
        in_specs=[VMEM] * 3,
        out_specs=(VMEM, VMEM),
        compiler_params=PARAMS,
        name="edges",
    )(ensemble, speed_row, speed_col)
    across = paired(across, "space", 1)
    within = paired(within, "space", 0)
    state = pl.pallas_call(
        advect_kernel,
        out_shape=f32(parts, rows, members, cols),
        in_specs=[VMEM] * 5,
        out_specs=VMEM,
        scratch_shapes=[pltpu.VMEM((rows + 2, 4, SUB, width), jnp.float32)],
        compiler_params=PARAMS,
        name="advect",
    )(planes, across, within, speed_row, speed_col)
    state = swap(state)
    tiles, centre = pl.pallas_call(
        tile_kernel,
        out_shape=(f32(per_patch, total + SUB, obs), f32(rows, cols)),
        in_specs=[SMEM] + [VMEM] * 4,
        out_specs=(VMEM, VMEM),
        compiler_params=PARAMS,
        name="tiles",
    )(obs_count[0, 0, 0], state, obs_cell[0, 0, 0], obs_value[0, 0, 0], obs_var[0, 0, 0])
    within = paired(tiles, "space", 0)
    across = paired(tiles, "space", 1)
    even_z = paired(tiles, "member", 0)
    odd_z = paired(tiles, "member", 1)
    within, across, even_z, odd_z = lax.optimization_barrier((within, across, even_z, odd_z))
    both_z = jnp.concatenate([even_z, odd_z])
    within_c = paired(both_z, "space", 0)
    across_c = paired(both_z, "space", 1)
    slots = loc_slots[0, 0, 0]
    state = pl.pallas_call(
        functools.partial(update, per_patch),
        out_shape=f32(parts, rows, members, cols),
        in_specs=[SMEM] + [VMEM] * 9,
        out_specs=VMEM,
        scratch_shapes=[
            pltpu.VMEM((total + SUB, slots.shape[0] * obs), jnp.float32),
            pltpu.VMEM((total, total), jnp.float32),
        ],
        compiler_params=PARAMS,
        name="update",
    )(slots, state, centre, tiles, odd_z, even_z, across, within, within_c, across_c)
    state = swap(state)
    return state.transpose(2, 1, 0, 3).reshape(members, rows, width)


def solution(mesh):
    return jax.shard_map(
        on_device,
        mesh=mesh,
        in_specs=(
            P("member", "space", None),
            P("space", None),
            P("space", None),
            P("space", "member", None, None, None),
            P("space", "member", None, None, None),
            P("space", "member", None, None, None),
            P("space", "member", None, None),
            P("space", "member", None, None),
        ),
        out_specs=P("member", "space", None),
        check_vma=False,
    )
```

```python
import functools

import jax
import jax.numpy as jnp
from jax import lax
from jax.experimental import pallas as pl
from jax.experimental.pallas import tpu as pltpu
from jax.sharding import PartitionSpec as P

K = 0.2
HI = lax.Precision.HIGHEST
SUB = 8
NT = (((1,), (1,)), ((), ()))


def split3(x):
    a = x.astype(jnp.bfloat16)
    rest = x - a.astype(jnp.float32)
    b = rest.astype(jnp.bfloat16)
    c = (rest - b.astype(jnp.float32)).astype(jnp.bfloat16)
    return a, b, c


def split2(x):
    a = x.astype(jnp.bfloat16)
    return a, (x - a.astype(jnp.float32)).astype(jnp.bfloat16)


def product(a, b, dims=(((1,), (0,)), ((), ()))):
    (a, a_low), (b, b_low) = a, b
    dot = functools.partial(
        lax.dot_general, dimension_numbers=dims, preferred_element_type=jnp.float32
    )
    return dot(a, b) + (dot(a, b_low) + dot(a_low, b))


def product3(a, b):
    return product(split2(a), split2(b))


def full(a, b):
    return jnp.dot(a, b, precision=HI)


def eye(n):
    rows = lax.broadcasted_iota(jnp.int32, (n, n), 0)
    cols = lax.broadcasted_iota(jnp.int32, (n, n), 1)
    return jnp.where(rows == cols, 1.0, 0.0).astype(jnp.float32)


def parity(axis):
    return lax.rem(lax.axis_index(axis), 2)


def edge_kernel(ensemble_far, row_far, col_far, across, within, ensemble, speed_row, speed_col, done):
    copies = [
        pltpu.make_async_copy(far, near, done.at[n])
        for n, (far, near) in enumerate(
            ((ensemble_far, ensemble), (row_far, speed_row), (col_far, speed_col))
        )
    ]
    for copy in copies:
        copy.start()
    for copy in copies:
        copy.wait()
    members, rows, width = ensemble.shape
    groups = members // SUB
    odd = parity("space") == 1

    def put(at, low, high):
        across[at] = jnp.where(odd, high, low)
        within[at] = jnp.where(odd, low, high)

    for g in range(groups):
        for n in range(2):
            low = ensemble[g * SUB : (g + 1) * SUB, n, :]
            high = ensemble[g * SUB : (g + 1) * SUB, rows - 2 + n, :]
            put(n * groups + g, low, high)
    across[2 * groups] = jnp.zeros((SUB, width), jnp.float32)
    within[2 * groups] = jnp.zeros((SUB, width), jnp.float32)
    for n, speed in enumerate((speed_row, speed_col)):
        put((2 * groups, slice(n, n + 1)), speed[0:1], speed[rows - 1 : rows])


def advect_kernel(planes, across, within, speed_row, speed_col, out, coef):
    rows, members, width = planes.shape
    blocks = out.shape[0]
    cols = out.shape[3]
    groups = members // SUB
    odd = parity("space") == 1

    def before(at):
        return jnp.where(odd, within[at], across[at])

    def after(at):
        return jnp.where(odd, across[at], within[at])

    top, bottom = before(2 * groups), after(2 * groups)
    for r in range(rows + 2):
        if r == 0:
            u, v = top[0:1], top[1:2]
        elif r == rows + 1:
            u, v = bottom[0:1], bottom[1:2]
        else:
            u, v = speed_row[r - 1 : r], speed_col[r - 1 : r]
        for n, c in enumerate((K + 0.5 * u, K - 0.5 * u, K + 0.5 * v, K - 0.5 * v)):
            coef[r, n] = jnp.broadcast_to(c, (SUB, width))

    def step(field, first):
        new = []
        for n in range(1, len(field) - 1):
            r = first + n - 1
            x = field[n]
            new.append(
                (1.0 - 4.0 * K) * x
                + coef[r, 0] * field[n - 1]
                + coef[r, 1] * field[n + 1]
                + coef[r, 2] * pltpu.roll(x, 1, 1)
                + coef[r, 3] * pltpu.roll(x, width - 1, 1)
            )
        return new

    def body(g, carry):
        at = pl.ds(pl.multiple_of(g * SUB, SUB), SUB)
        field = [before(g), before(groups + g)]
        field += [planes[i, at, :] for i in range(rows)]
        field += [after(g), after(groups + g)]
        field = step(step(field, 0), 1)
        for i in range(rows):
            for b in range(blocks):
                out[b, i, at, :] = field[i][:, b * cols : (b + 1) * cols]
        return carry

    lax.fori_loop(0, groups, body, 0)


def patch_matrix(state):
    parts, rows, members, cols = state.shape
    return jnp.concatenate(
        [state[:, i].reshape(parts * members, cols) for i in range(rows)], axis=1
    )


def tile_kernel(count, state, cell, value, variance, tiles, centre):
    parts, rows, members, cols = state.shape
    total = parts * members
    cells = rows * cols
    per_patch, obs = cell.shape
    x = patch_matrix(state)
    mean = jnp.sum(x, axis=0, keepdims=True) * (1.0 / total)
    for i in range(rows):
        centre[i : i + 1, :] = mean[:, i * cols : (i + 1) * cols]
    anomaly = jnp.concatenate([x - mean, jnp.broadcast_to(mean, (SUB, cells))], axis=0)
    parts3 = split3(anomaly)
    row = lax.broadcasted_iota(jnp.int32, (cells, obs), 0)
    lane = lax.broadcasted_iota(jnp.int32, (1, obs), 1)
    below = lax.broadcasted_iota(jnp.int32, (SUB, obs), 0)
    for t in range(per_patch):
        pick = jnp.where(row == cell[t : t + 1, :], 1.0, 0.0).astype(jnp.bfloat16)
        y = sum(jnp.dot(p, pick, preferred_element_type=jnp.float32) for p in parts3[::-1])
        live = lane < count[t]
        weight = jnp.where(live, 1.0 / variance[t : t + 1, :], 0.0)
        scale = jnp.sqrt(weight * (1.0 / (total - 1.0)))
        tiles[t, 0:total, :] = y[:total] * scale
        innovation = (value[t : t + 1, :] - y[total:]) * scale
        tiles[t, total : total + SUB, :] = jnp.where(below == 0, innovation, 0.0)


def spd_inverse(s):
    n = s.shape[0]
    unit = eye(n)
    size = jnp.sum(s * s)
    bound = jnp.minimum(jnp.sqrt(size), jnp.max(jnp.sum(jnp.abs(s), axis=0)))
    bound = jnp.maximum(bound, 1.0) * 1.0001
    scale = 2.0 / (1.0 + bound)
    x = scale * unit
    e = unit - scale * s
    rho = (bound - 1.0) / (bound + 1.0)

    def square(multiply, carry):
        x, e, rho = carry
        both = multiply(jnp.concatenate([x, e], axis=0), e)
        square_rho = rho * rho
        scale = 2.0 / (2.0 - square_rho)
        x = scale * (x + both[:n])
        e = scale * both[n:] + (1.0 - scale) * unit
        return x, e, square_rho / (2.0 - square_rho)

    def quick(carry):
        return (carry[2] > 1e-3) & (bound < 1000.0)

    def careful(carry):
        return carry[2] > 1e-3

    carry = lax.while_loop(quick, functools.partial(square, product3), (x, e, rho))
    x = lax.while_loop(careful, functools.partial(square, full), carry)[0]

    def unsettled(carry):
        return (carry[1] > 1e-5) & (carry[2] < 8)

    def newton(carry):
        x, _, count = carry
        e = unit - full(s, x)
        return x + product3(x, e), jnp.sum(e * e), count + 1

    return lax.while_loop(unsettled, newton, (x, jnp.float32(1.0), jnp.int32(0)))[0]


def update_kernel(per_patch, slots, state, centre, lines, corners, out, z, inv):
    parts, rows, members, cols = state.shape
    total = parts * members
    half = total // 2
    odd_row, odd_col = parity("space"), parity("member")
    mask = jnp.int32(0)
    for n in range(slots.shape[0]):
        o, t = lax.div(slots[n], per_patch), lax.rem(slots[n], per_patch)
        r, s = lax.div(o, 3), lax.rem(o, 3)
        r = r + odd_row * (2 - 2 * r)
        s = s + odd_col * (2 - 2 * s)
        mask = mask | lax.shift_left(jnp.int32(1), (r * 3 + s) * per_patch + t)
    place = jnp.int32(0)
    for q in range(9 * per_patch):
        o, t = q // per_patch, q % per_patch
        r, s = o // 3 - 1, o % 3 - 1
        taper = 1.0 / (1.0 + r * r + s * s)
        chosen = lax.shift_right_logical(mask, q) & 1
        ref = corners[r, s][0] if r and s else lines[r, s]
        row = t + (corners[r, s][1] if r and s else 0)

        @pl.when(chosen == 1)
        def _():
            obs = ref.shape[2]
            z[:, pl.ds(pl.multiple_of(place * obs, obs), obs)] = ref[row] * (taper**0.5)

        place = place + chosen
    z1, z2 = split2(z[0:half, :]), split2(z[half:total, :])
    zd = split2(z[total:, :])
    top = [jnp.concatenate([p, q], axis=0) for p, q in zip(z1, zd)]
    gram1 = product(top, z1, NT)
    gram2 = product(top, z2, NT)
    drive = jnp.concatenate([gram1[half:], gram2[half:]], axis=1)
    s11 = gram1[:half] + eye(half)
    s12 = gram2[:half]
    s22 = product(z2, z2, NT) + eye(half)
    inv11 = spd_inverse(s11)
    w = jnp.dot(inv11, s12, precision=HI)
    schur = s22 - lax.dot_general(s12, w, (((0,), (0,)), ((), ())), precision=HI)
    inv22 = spd_inverse(0.5 * (schur + schur.T))
    low = jnp.dot(w, inv22, precision=HI)
    inv[0:half, 0:half] = inv11 + lax.dot_general(low, w, NT, precision=HI)
    inv[0:half, half:] = -low
    inv[half:, 0:half] = -low.T
    inv[half:, half:] = inv22
    shift = jnp.dot(drive, inv[...], precision=HI)[0:1]
    mean = jnp.concatenate([centre[i : i + 1, :] for i in range(rows)], axis=1)
    anomaly = patch_matrix(state) - mean
    result = product3(0.5 * inv[...] + shift, anomaly)
    result = result + (mean + 0.5 * anomaly)
    for p in range(parts):
        for i in range(rows):
            out[p, i] = result[p * members : (p + 1) * members, i * cols : (i + 1) * cols]


def update(per_patch, slots, state, centre, own, odd_z, even_z, across, within, within_c, across_c, *rest):
    lines = {(0, 0): own, (0, 1): even_z, (0, -1): odd_z, (-1, 0): across, (1, 0): within}
    corners = {
        (-1, 1): (across_c, 0),
        (-1, -1): (across_c, per_patch),
        (1, 1): (within_c, 0),
        (1, -1): (within_c, per_patch),
    }
    update_kernel(per_patch, slots, state, centre, lines, corners, *rest)


VMEM = pl.BlockSpec(memory_space=pltpu.VMEM)
SMEM = pl.BlockSpec(memory_space=pltpu.SMEM)
PARAMS = pltpu.CompilerParams(vmem_limit_bytes=28 * 1024 * 1024)


def f32(*shape):
    return jax.ShapeDtypeStruct(shape, jnp.float32)


def paired(x, axis, first):
    n = lax.axis_size(axis)
    pairs = [(i, (i + 1) % n) for i in range(first, n, 2)]
    return lax.ppermute(x, axis, pairs + [(j, i) for i, j in pairs])


def swap(x):
    return lax.all_to_all(x, "member", split_axis=0, concat_axis=0, tiled=True)


def on_device(ensemble, speed_row, speed_col, obs_cell, obs_value, obs_var, obs_count, loc_slots):
    members, rows, width = ensemble.shape
    parts = lax.axis_size("member")
    cols = width // parts
    groups = members // SUB
    per_patch, obs = obs_cell.shape[3:]
    total = parts * members

    planes = ensemble.transpose(1, 0, 2)
    across, within = pl.pallas_call(
        edge_kernel,
        out_shape=(f32(2 * groups + 1, SUB, width), f32(2 * groups + 1, SUB, width)),
        in_specs=[pl.BlockSpec(memory_space=pltpu.HBM)] * 3,
        out_specs=(VMEM, VMEM),
        scratch_shapes=[
            pltpu.VMEM(ensemble.shape, jnp.float32),
            pltpu.VMEM(speed_row.shape, jnp.float32),
            pltpu.VMEM(speed_col.shape, jnp.float32),
            pltpu.SemaphoreType.DMA((3,)),
        ],
        compiler_params=pltpu.CompilerParams(vmem_limit_bytes=62 * 1024 * 1024),
        name="edges",
    )(ensemble, speed_row, speed_col)
    across = paired(across, "space", 1)
    within = paired(within, "space", 0)
    state = pl.pallas_call(
        advect_kernel,
        out_shape=f32(parts, rows, members, cols),
        in_specs=[VMEM] * 5,
        out_specs=VMEM,
        scratch_shapes=[pltpu.VMEM((rows + 2, 4, SUB, width), jnp.float32)],
        compiler_params=PARAMS,
        name="advect",
    )(planes, across, within, speed_row, speed_col)
    state = swap(state)
    tiles, centre = pl.pallas_call(
        tile_kernel,
        out_shape=(f32(per_patch, total + SUB, obs), f32(rows, cols)),
        in_specs=[SMEM] + [VMEM] * 4,
        out_specs=(VMEM, VMEM),
        compiler_params=PARAMS,
        name="tiles",
    )(obs_count[0, 0, 0], state, obs_cell[0, 0, 0], obs_value[0, 0, 0], obs_var[0, 0, 0])
    within = paired(tiles, "space", 0)
    across = paired(tiles, "space", 1)
    even_z = paired(tiles, "member", 0)
    odd_z = paired(tiles, "member", 1)
    within, across, even_z, odd_z = lax.optimization_barrier((within, across, even_z, odd_z))
    both_z = jnp.concatenate([even_z, odd_z])
    within_c = paired(both_z, "space", 0)
    across_c = paired(both_z, "space", 1)
    slots = loc_slots[0, 0, 0]
    state = pl.pallas_call(
        functools.partial(update, per_patch),
        out_shape=f32(parts, rows, members, cols),
        in_specs=[SMEM] + [VMEM] * 9,
        out_specs=VMEM,
        scratch_shapes=[
            pltpu.VMEM((total + SUB, slots.shape[0] * obs), jnp.float32),
            pltpu.VMEM((total, total), jnp.float32),
        ],
        compiler_params=PARAMS,
        name="update",
    )(slots, state, centre, tiles, odd_z, even_z, across, within, within_c, across_c)
    state = swap(state)
    return state.transpose(2, 1, 0, 3).reshape(members, rows, width)


def solution(mesh):
    return jax.shard_map(
        on_device,
        mesh=mesh,
        in_specs=(
            P("member", "space", None),
            P("space", None),
            P("space", None),
            P("space", "member", None, None, None),
            P("space", "member", None, None, None),
            P("space", "member", None, None, None),
            P("space", "member", None, None),
            P("space", "member", None, None),
        ),
        out_specs=P("member", "space", None),
        check_vma=False,
    )
```

```python
import functools

import jax
import jax.numpy as jnp
from jax import lax
from jax.experimental import pallas as pl
from jax.experimental.pallas import tpu as pltpu
from jax.sharding import PartitionSpec as P

K = 0.2
HI = lax.Precision.HIGHEST
SUB = 8
NT = (((1,), (1,)), ((), ()))


def split3(x):
    a = x.astype(jnp.bfloat16)
    rest = x - a.astype(jnp.float32)
    b = rest.astype(jnp.bfloat16)
    c = (rest - b.astype(jnp.float32)).astype(jnp.bfloat16)
    return a, b, c


def split2(x):
    a = x.astype(jnp.bfloat16)
    return a, (x - a.astype(jnp.float32)).astype(jnp.bfloat16)


def product(a, b, dims=(((1,), (0,)), ((), ()))):
    (a, a_low), (b, b_low) = a, b
    dot = functools.partial(
        lax.dot_general, dimension_numbers=dims, preferred_element_type=jnp.float32
    )
    return dot(a, b) + (dot(a, b_low) + dot(a_low, b))


def product3(a, b):
    return product(split2(a), split2(b))


def full(a, b):
    return jnp.dot(a, b, precision=HI)


def eye(n):
    rows = lax.broadcasted_iota(jnp.int32, (n, n), 0)
    cols = lax.broadcasted_iota(jnp.int32, (n, n), 1)
    return jnp.where(rows == cols, 1.0, 0.0).astype(jnp.float32)


def parity(axis):
    return lax.rem(lax.axis_index(axis), 2)


def edge_kernel(ensemble_far, row_far, col_far, across, within, ensemble, speed_row, speed_col, done):
    members, rows, width = ensemble.shape
    groups = members // SUB
    odd = parity("space") == 1

    def fetch(far, near, n):
        return pltpu.make_async_copy(far, near, done.at[n])

    def part(g):
        at = pl.ds(g * SUB, SUB)
        return fetch(ensemble_far.at[at], ensemble.at[at], g)

    copies = [part(g) for g in range(groups)]
    copies += [fetch(row_far, speed_row, groups), fetch(col_far, speed_col, groups + 1)]
    for copy in copies:
        copy.start()

    def put(at, low, high):
        across[at] = jnp.where(odd, high, low)
        within[at] = jnp.where(odd, low, high)

    for g in range(groups):
        copies[g].wait()
        for n in range(2):
            low = ensemble[g * SUB : (g + 1) * SUB, n, :]
            high = ensemble[g * SUB : (g + 1) * SUB, rows - 2 + n, :]
            put(n * groups + g, low, high)
    across[2 * groups] = jnp.zeros((SUB, width), jnp.float32)
    within[2 * groups] = jnp.zeros((SUB, width), jnp.float32)
    for n, speed in enumerate((speed_row, speed_col)):
        copies[groups + n].wait()
        put((2 * groups, slice(n, n + 1)), speed[0:1], speed[rows - 1 : rows])


def advect_kernel(planes, across, within, speed_row, speed_col, out, coef):
    rows, members, width = planes.shape
    blocks = out.shape[0]
    cols = out.shape[3]
    groups = members // SUB
    odd = parity("space") == 1

    def before(at):
        return jnp.where(odd, within[at], across[at])

    def after(at):
        return jnp.where(odd, across[at], within[at])

    top, bottom = before(2 * groups), after(2 * groups)
    for r in range(rows + 2):
        if r == 0:
            u, v = top[0:1], top[1:2]
        elif r == rows + 1:
            u, v = bottom[0:1], bottom[1:2]
        else:
            u, v = speed_row[r - 1 : r], speed_col[r - 1 : r]
        for n, c in enumerate((K + 0.5 * u, K - 0.5 * u, K + 0.5 * v, K - 0.5 * v)):
            coef[r, n] = jnp.broadcast_to(c, (SUB, width))

    def step(field, first):
        new = []
        for n in range(1, len(field) - 1):
            r = first + n - 1
            x = field[n]
            new.append(
                (1.0 - 4.0 * K) * x
                + coef[r, 0] * field[n - 1]
                + coef[r, 1] * field[n + 1]
                + coef[r, 2] * pltpu.roll(x, 1, 1)
                + coef[r, 3] * pltpu.roll(x, width - 1, 1)
            )
        return new

    def body(g, carry):
        at = pl.ds(pl.multiple_of(g * SUB, SUB), SUB)
        field = [before(g), before(groups + g)]
        field += [planes[i, at, :] for i in range(rows)]
        field += [after(g), after(groups + g)]
        field = step(step(field, 0), 1)
        for i in range(rows):
            for b in range(blocks):
                out[b, i, at, :] = field[i][:, b * cols : (b + 1) * cols]
        return carry

    lax.fori_loop(0, groups, body, 0)


def patch_matrix(state):
    parts, rows, members, cols = state.shape
    return jnp.concatenate(
        [state[:, i].reshape(parts * members, cols) for i in range(rows)], axis=1
    )


def tile_kernel(count, state, cell, value, variance, tiles, centre):
    parts, rows, members, cols = state.shape
    total = parts * members
    cells = rows * cols
    per_patch, obs = cell.shape
    x = patch_matrix(state)
    mean = jnp.sum(x, axis=0, keepdims=True) * (1.0 / total)
    for i in range(rows):
        centre[i : i + 1, :] = mean[:, i * cols : (i + 1) * cols]
    anomaly = jnp.concatenate([x - mean, jnp.broadcast_to(mean, (SUB, cells))], axis=0)
    parts3 = split3(anomaly)
    row = lax.broadcasted_iota(jnp.int32, (cells, obs), 0)
    lane = lax.broadcasted_iota(jnp.int32, (1, obs), 1)
    below = lax.broadcasted_iota(jnp.int32, (SUB, obs), 0)
    for t in range(per_patch):
        pick = jnp.where(row == cell[t : t + 1, :], 1.0, 0.0).astype(jnp.bfloat16)
        y = sum(jnp.dot(p, pick, preferred_element_type=jnp.float32) for p in parts3[::-1])
        live = lane < count[t]
        weight = jnp.where(live, 1.0 / variance[t : t + 1, :], 0.0)
        scale = jnp.sqrt(weight * (1.0 / (total - 1.0)))
        tiles[t, 0:total, :] = y[:total] * scale
        innovation = (value[t : t + 1, :] - y[total:]) * scale
        tiles[t, total : total + SUB, :] = jnp.where(below == 0, innovation, 0.0)


def spd_inverse(s):
    n = s.shape[0]
    unit = eye(n)
    size = jnp.sum(s * s)
    bound = jnp.minimum(jnp.sqrt(size), jnp.max(jnp.sum(jnp.abs(s), axis=0)))
    bound = jnp.maximum(bound, 1.0) * 1.0001
    scale = 2.0 / (1.0 + bound)
    x = scale * unit
    e = unit - scale * s
    rho = (bound - 1.0) / (bound + 1.0)

    def square(multiply, carry):
        x, e, rho = carry
        both = multiply(jnp.concatenate([x, e], axis=0), e)
        square_rho = rho * rho
        scale = 2.0 / (2.0 - square_rho)
        x = scale * (x + both[:n])
        e = scale * both[n:] + (1.0 - scale) * unit
        return x, e, square_rho / (2.0 - square_rho)

    def quick(carry):
        return (carry[2] > 1e-3) & (bound < 1000.0)

    def careful(carry):
        return carry[2] > 1e-3

    carry = lax.while_loop(quick, functools.partial(square, product3), (x, e, rho))
    x = lax.while_loop(careful, functools.partial(square, full), carry)[0]

    def unsettled(carry):
        return (carry[1] > 1e-5) & (carry[2] < 8)

    def newton(carry):
        x, _, count = carry
        e = unit - full(s, x)
        return x + product3(x, e), jnp.sum(e * e), count + 1

    return lax.while_loop(unsettled, newton, (x, jnp.float32(1.0), jnp.int32(0)))[0]


def fill(z, slots, per_patch, tiles):
    odd_row, odd_col = parity("space"), parity("member")
    mask = jnp.int32(0)
    for n in range(slots.shape[0]):
        o, t = lax.div(slots[n], per_patch), lax.rem(slots[n], per_patch)
        r, s = lax.div(o, 3), lax.rem(o, 3)
        r = r + odd_row * (2 - 2 * r)
        s = s + odd_col * (2 - 2 * s)
        mask = mask | lax.shift_left(jnp.int32(1), (r * 3 + s) * per_patch + t)
    for n, (r, s, ref, first) in enumerate(tiles):
        for t in range(per_patch):
            bit = ((r + 1) * 3 + s + 1) * per_patch + t
            chosen = (lax.shift_right_logical(mask, bit) & 1).astype(jnp.float32)
            root = (1.0 / (1.0 + r * r + s * s)) ** 0.5
            obs = ref.shape[2]
            at = (n * per_patch + t) * obs
            z[:, at : at + obs] = ref[first + t] * (chosen * root)


def gram_blocks(z, total):
    half = total // 2
    z1, z2 = split2(z[0:half, :]), split2(z[half:total, :])
    zd = split2(z[total:, :])
    top = [jnp.concatenate([p, q], axis=0) for p, q in zip(z1, zd)]
    return product(top, z1, NT), product(top, z2, NT), product(z2, z2, NT)


def near_kernel(per_patch, slots, own, odd_z, even_z, within, across, gram1, gram2, gram3, z):
    tiles = ((0, 0, own, 0), (0, -1, odd_z, 0), (0, 1, even_z, 0), (-1, 0, across, 0), (1, 0, within, 0))
    fill(z, slots, per_patch, tiles)
    gram1[...], gram2[...], gram3[...] = gram_blocks(z, 2 * gram3.shape[0])


def update_kernel(per_patch, slots, state, centre, near1, near2, near3, within, across, out, z, inv):
    parts, rows, members, cols = state.shape
    total = parts * members
    half = total // 2
    tiles = (
        (-1, 1, across, 0),
        (-1, -1, across, per_patch),
        (1, 1, within, 0),
        (1, -1, within, per_patch),
    )
    fill(z, slots, per_patch, tiles)
    gram1, gram2, gram3 = gram_blocks(z, total)
    gram1, gram2 = gram1 + near1[...], gram2 + near2[...]
    drive = jnp.concatenate([gram1[half:], gram2[half:]], axis=1)
    s11 = gram1[:half] + eye(half)
    s12 = gram2[:half]
    s22 = gram3 + near3[...] + eye(half)
    inv11 = spd_inverse(s11)
    w = jnp.dot(inv11, s12, precision=HI)
    schur = s22 - lax.dot_general(s12, w, (((0,), (0,)), ((), ())), precision=HI)
    inv22 = spd_inverse(0.5 * (schur + schur.T))
    low = jnp.dot(w, inv22, precision=HI)
    inv[0:half, 0:half] = inv11 + lax.dot_general(low, w, NT, precision=HI)
    inv[0:half, half:] = -low
    inv[half:, 0:half] = -low.T
    inv[half:, half:] = inv22
    shift = jnp.dot(drive, inv[...], precision=HI)[0:1]
    mean = jnp.concatenate([centre[i : i + 1, :] for i in range(rows)], axis=1)
    anomaly = patch_matrix(state) - mean
    result = product3(0.5 * inv[...] + shift, anomaly)
    result = result + (mean + 0.5 * anomaly)
    for p in range(parts):
        for i in range(rows):
            out[p, i] = result[p * members : (p + 1) * members, i * cols : (i + 1) * cols]


VMEM = pl.BlockSpec(memory_space=pltpu.VMEM)
SMEM = pl.BlockSpec(memory_space=pltpu.SMEM)
PARAMS = pltpu.CompilerParams(vmem_limit_bytes=28 * 1024 * 1024)


def f32(*shape):
    return jax.ShapeDtypeStruct(shape, jnp.float32)


def paired(x, axis, first):
    n = lax.axis_size(axis)
    pairs = [(i, (i + 1) % n) for i in range(first, n, 2)]
    return lax.ppermute(x, axis, pairs + [(j, i) for i, j in pairs])


def swap(x):
    return lax.all_to_all(x, "member", split_axis=0, concat_axis=0, tiled=True)


def on_device(ensemble, speed_row, speed_col, obs_cell, obs_value, obs_var, obs_count, loc_slots):
    members, rows, width = ensemble.shape
    parts = lax.axis_size("member")
    cols = width // parts
    groups = members // SUB
    per_patch, obs = obs_cell.shape[3:]
    total = parts * members

    planes = ensemble.transpose(1, 0, 2)
    across, within = pl.pallas_call(
        edge_kernel,
        out_shape=(f32(2 * groups + 1, SUB, width), f32(2 * groups + 1, SUB, width)),
        in_specs=[pl.BlockSpec(memory_space=pltpu.HBM)] * 3,
        out_specs=(VMEM, VMEM),
        scratch_shapes=[
            pltpu.VMEM(ensemble.shape, jnp.float32),
            pltpu.VMEM(speed_row.shape, jnp.float32),
            pltpu.VMEM(speed_col.shape, jnp.float32),
            pltpu.SemaphoreType.DMA((groups + 2,)),
        ],
        compiler_params=pltpu.CompilerParams(vmem_limit_bytes=62 * 1024 * 1024),
        name="edges",
    )(ensemble, speed_row, speed_col)
    across = paired(across, "space", 1)
    within = paired(within, "space", 0)
    state = pl.pallas_call(
        advect_kernel,
        out_shape=f32(parts, rows, members, cols),
        in_specs=[VMEM] * 5,
        out_specs=VMEM,
        scratch_shapes=[pltpu.VMEM((rows + 2, 4, SUB, width), jnp.float32)],
        compiler_params=PARAMS,
        name="advect",
    )(planes, across, within, speed_row, speed_col)
    state = swap(state)
    tiles, centre = pl.pallas_call(
        tile_kernel,
        out_shape=(f32(per_patch, total + SUB, obs), f32(rows, cols)),
        in_specs=[SMEM] + [VMEM] * 4,
        out_specs=(VMEM, VMEM),
        compiler_params=PARAMS,
        name="tiles",
    )(obs_count[0, 0, 0], state, obs_cell[0, 0, 0], obs_value[0, 0, 0], obs_var[0, 0, 0])
    within = paired(tiles, "space", 0)
    across = paired(tiles, "space", 1)
    even_z = paired(tiles, "member", 0)
    odd_z = paired(tiles, "member", 1)
    both_z = jnp.concatenate([even_z, odd_z])
    within_c = paired(both_z, "space", 0)
    across_c = paired(both_z, "space", 1)
    slots = loc_slots[0, 0, 0]
    half = total // 2
    depth = per_patch * obs
    near = pl.pallas_call(
        functools.partial(near_kernel, per_patch),
        out_shape=(f32(half + SUB, half), f32(half + SUB, half), f32(half, half)),
        in_specs=[SMEM] + [VMEM] * 5,
        out_specs=(VMEM, VMEM, VMEM),
        scratch_shapes=[pltpu.VMEM((total + SUB, 5 * depth), jnp.float32)],
        compiler_params=PARAMS,
        cost_estimate=pl.CostEstimate(
            flops=240 * total * total * depth, bytes_accessed=12 * (total + SUB) * depth * 4, transcendentals=0
        ),
        name="near_gram",
    )(slots, tiles, odd_z, even_z, within, across)
    state = pl.pallas_call(
        functools.partial(update_kernel, per_patch),
        out_shape=f32(parts, rows, members, cols),
        in_specs=[SMEM] + [VMEM] * 7,
        out_specs=VMEM,
        scratch_shapes=[
            pltpu.VMEM((total + SUB, 4 * depth), jnp.float32),
            pltpu.VMEM((total, total), jnp.float32),
        ],
        compiler_params=PARAMS,
        name="update",
    )(slots, state, centre, *near, within_c, across_c)
    state = swap(state)
    return state.transpose(2, 1, 0, 3).reshape(members, rows, width)


def solution(mesh):
    return jax.shard_map(
        on_device,
        mesh=mesh,
        in_specs=(
            P("member", "space", None),
            P("space", None),
            P("space", None),
            P("space", "member", None, None, None),
            P("space", "member", None, None, None),
            P("space", "member", None, None, None),
            P("space", "member", None, None),
            P("space", "member", None, None),
        ),
        out_specs=P("member", "space", None),
        check_vma=False,
    )
```

```python
import functools

import jax
import jax.numpy as jnp
from jax import lax
from jax.experimental import pallas as pl
from jax.experimental.pallas import tpu as pltpu
from jax.sharding import PartitionSpec as P

K = 0.2
HI = lax.Precision.HIGHEST
SUB = 8
NT = (((1,), (1,)), ((), ()))


def split3(x):
    a = x.astype(jnp.bfloat16)
    rest = x - a.astype(jnp.float32)
    b = rest.astype(jnp.bfloat16)
    c = (rest - b.astype(jnp.float32)).astype(jnp.bfloat16)
    return a, b, c


def split2(x):
    a = x.astype(jnp.bfloat16)
    return a, (x - a.astype(jnp.float32)).astype(jnp.bfloat16)


def product(a, b, dims=(((1,), (0,)), ((), ()))):
    (a, a_low), (b, b_low) = a, b
    dot = functools.partial(
        lax.dot_general, dimension_numbers=dims, preferred_element_type=jnp.float32
    )
    return dot(a, b) + (dot(a, b_low) + dot(a_low, b))


def product3(a, b):
    return product(split2(a), split2(b))


def full(a, b):
    return jnp.dot(a, b, precision=HI)


def eye(n):
    rows = lax.broadcasted_iota(jnp.int32, (n, n), 0)
    cols = lax.broadcasted_iota(jnp.int32, (n, n), 1)
    return jnp.where(rows == cols, 1.0, 0.0).astype(jnp.float32)


def parity(axis):
    return lax.rem(lax.axis_index(axis), 2)


def edge_kernel(ensemble_far, row_far, col_far, across, within, ensemble, speed_row, speed_col, done):
    members, rows, width = ensemble.shape
    groups = members // SUB
    odd = parity("space") == 1

    def fetch(far, near, n):
        return pltpu.make_async_copy(far, near, done.at[n])

    def part(g):
        at = pl.ds(g * SUB, SUB)
        return fetch(ensemble_far.at[at], ensemble.at[at], g)

    copies = [part(g) for g in range(groups)]
    copies += [fetch(row_far, speed_row, groups), fetch(col_far, speed_col, groups + 1)]
    for copy in copies:
        copy.start()

    def put(at, low, high):
        across[at] = jnp.where(odd, high, low)
        within[at] = jnp.where(odd, low, high)

    for g in range(groups):
        copies[g].wait()
        for n in range(2):
            low = ensemble[g * SUB : (g + 1) * SUB, n, :]
            high = ensemble[g * SUB : (g + 1) * SUB, rows - 2 + n, :]
            put(n * groups + g, low, high)
    across[2 * groups] = jnp.zeros((SUB, width), jnp.float32)
    within[2 * groups] = jnp.zeros((SUB, width), jnp.float32)
    for n, speed in enumerate((speed_row, speed_col)):
        copies[groups + n].wait()
        put((2 * groups, slice(n, n + 1)), speed[0:1], speed[rows - 1 : rows])


def advect_kernel(planes, across, within, speed_row, speed_col, out, coef):
    rows, members, width = planes.shape
    blocks = out.shape[0]
    cols = out.shape[3]
    groups = members // SUB
    odd = parity("space") == 1

    def before(at):
        return jnp.where(odd, within[at], across[at])

    def after(at):
        return jnp.where(odd, across[at], within[at])

    top, bottom = before(2 * groups), after(2 * groups)
    for r in range(rows + 2):
        if r == 0:
            u, v = top[0:1], top[1:2]
        elif r == rows + 1:
            u, v = bottom[0:1], bottom[1:2]
        else:
            u, v = speed_row[r - 1 : r], speed_col[r - 1 : r]
        for n, c in enumerate((K + 0.5 * u, K - 0.5 * u, K + 0.5 * v, K - 0.5 * v)):
            coef[r, n] = jnp.broadcast_to(c, (SUB, width))

    def step(field, first):
        new = []
        for n in range(1, len(field) - 1):
            r = first + n - 1
            x = field[n]
            new.append(
                (1.0 - 4.0 * K) * x
                + coef[r, 0] * field[n - 1]
                + coef[r, 1] * field[n + 1]
                + coef[r, 2] * pltpu.roll(x, 1, 1)
                + coef[r, 3] * pltpu.roll(x, width - 1, 1)
            )
        return new

    def body(g, carry):
        at = pl.ds(pl.multiple_of(g * SUB, SUB), SUB)
        field = [before(g), before(groups + g)]
        field += [planes[i, at, :] for i in range(rows)]
        field += [after(g), after(groups + g)]
        field = step(step(field, 0), 1)
        for i in range(rows):
            for b in range(blocks):
                out[b, i, at, :] = field[i][:, b * cols : (b + 1) * cols]
        return carry

    lax.fori_loop(0, groups, body, 0)


def patch_matrix(state):
    parts, rows, members, cols = state.shape
    return jnp.concatenate(
        [state[:, i].reshape(parts * members, cols) for i in range(rows)], axis=1
    )


def gather_kernel(state, cell, raw):
    blocks, rows, members, cols = state.shape
    per_patch, obs = cell.shape[1:]
    row = lax.broadcasted_iota(jnp.int32, (rows * cols, obs), 0)
    for b in range(blocks):
        x = jnp.concatenate([state[b, i] for i in range(rows)], axis=1)
        x = jnp.concatenate(split3(x)[::-1], axis=0)
        pick = [jnp.where(row == cell[b, t : t + 1, :], 1.0, 0.0) for t in range(per_patch)]
        pick = jnp.concatenate(pick, axis=1).astype(jnp.bfloat16)
        y = jnp.dot(x, pick, preferred_element_type=jnp.float32)
        y = y[:members] + y[members : 2 * members] + y[2 * members :]
        for t in range(per_patch):
            raw[b, t] = y[:, t * obs : (t + 1) * obs]


def tile_kernel(count, raw, value, variance, tiles):
    parts, per_patch, members, obs = raw.shape
    total = parts * members
    lane = lax.broadcasted_iota(jnp.int32, (1, obs), 1)
    below = lax.broadcasted_iota(jnp.int32, (SUB, obs), 0)
    for t in range(per_patch):
        y = raw[:, t].reshape(total, obs)
        mean = jnp.sum(y, axis=0, keepdims=True) * (1.0 / total)
        weight = jnp.where(lane < count[t], 1.0 / variance[t : t + 1, :], 0.0)
        scale = jnp.sqrt(weight * (1.0 / (total - 1.0)))
        tiles[t, 0:total, :] = (y - mean) * scale
        innovation = (value[t : t + 1, :] - mean) * scale
        tiles[t, total : total + SUB, :] = jnp.where(below == 0, innovation, 0.0)


def spd_inverse(s):
    n = s.shape[0]
    unit = eye(n)
    size = jnp.sum(s * s)
    bound = jnp.minimum(jnp.sqrt(size), jnp.max(jnp.sum(jnp.abs(s), axis=0)))
    bound = jnp.maximum(bound, 1.0) * 1.0001
    scale = 2.0 / (1.0 + bound)
    x = scale * unit
    e = unit - scale * s
    rho = (bound - 1.0) / (bound + 1.0)

    def square(multiply, carry):
        x, e, rho = carry
        both = multiply(jnp.concatenate([x, e], axis=0), e)
        square_rho = rho * rho
        scale = 2.0 / (2.0 - square_rho)
        x = scale * (x + both[:n])
        e = scale * both[n:] + (1.0 - scale) * unit
        return x, e, square_rho / (2.0 - square_rho)

    def quick(carry):
        return (carry[2] > 1e-3) & (bound < 1000.0)

    def careful(carry):
        return carry[2] > 1e-3

    carry = lax.while_loop(quick, functools.partial(square, product3), (x, e, rho))
    x = lax.while_loop(careful, functools.partial(square, full), carry)[0]

    def unsettled(carry):
        return (carry[1] > 1e-5) & (carry[2] < 8)

    def newton(carry):
        x, _, count = carry
        e = unit - full(s, x)
        return x + product3(x, e), jnp.sum(e * e), count + 1

    return lax.while_loop(unsettled, newton, (x, jnp.float32(1.0), jnp.int32(0)))[0]


def fill(z, slots, per_patch, tiles):
    odd_row, odd_col = parity("space"), parity("member")
    mask = jnp.int32(0)
    for n in range(slots.shape[0]):
        o, t = lax.div(slots[n], per_patch), lax.rem(slots[n], per_patch)
        r, s = lax.div(o, 3), lax.rem(o, 3)
        r = r + odd_row * (2 - 2 * r)
        s = s + odd_col * (2 - 2 * s)
        mask = mask | lax.shift_left(jnp.int32(1), (r * 3 + s) * per_patch + t)
    for n, (r, s, ref, first) in enumerate(tiles):
        for t in range(per_patch):
            bit = ((r + 1) * 3 + s + 1) * per_patch + t
            chosen = (lax.shift_right_logical(mask, bit) & 1).astype(jnp.float32)
            root = (1.0 / (1.0 + r * r + s * s)) ** 0.5
            obs = ref.shape[2]
            at = (n * per_patch + t) * obs
            z[:, at : at + obs] = ref[first + t] * (chosen * root)


def gram_blocks(z, total):
    half = total // 2
    z1, z2 = split2(z[0:half, :]), split2(z[half:total, :])
    zd = split2(z[total:, :])
    top = [jnp.concatenate([p, q], axis=0) for p, q in zip(z1, zd)]
    return product(top, z1, NT), product(top, z2, NT), product(z2, z2, NT)


def near_kernel(per_patch, slots, own, odd_z, even_z, within, across, gram1, gram2, gram3, z):
    tiles = ((0, 0, own, 0), (0, -1, odd_z, 0), (0, 1, even_z, 0), (-1, 0, across, 0), (1, 0, within, 0))
    fill(z, slots, per_patch, tiles)
    gram1[...], gram2[...], gram3[...] = gram_blocks(z, 2 * gram3.shape[0])


def weight_kernel(per_patch, slots, near1, near2, near3, within, across, out, z):
    half = near3.shape[0]
    total = 2 * half
    tiles = (
        (-1, 1, across, 0),
        (-1, -1, across, per_patch),
        (1, 1, within, 0),
        (1, -1, within, per_patch),
    )
    fill(z, slots, per_patch, tiles)
    gram1, gram2, gram3 = gram_blocks(z, total)
    gram1, gram2 = gram1 + near1[...], gram2 + near2[...]
    drive = jnp.concatenate([gram1[half:], gram2[half:]], axis=1)
    s11 = gram1[:half] + eye(half)
    s12 = gram2[:half]
    s22 = gram3 + near3[...] + eye(half)
    inv11 = spd_inverse(s11)
    w = jnp.dot(inv11, s12, precision=HI)
    schur = s22 - lax.dot_general(s12, w, (((0,), (0,)), ((), ())), precision=HI)
    inv22 = spd_inverse(0.5 * (schur + schur.T))
    low = jnp.dot(w, inv22, precision=HI)
    inv = jnp.concatenate(
        [
            jnp.concatenate([inv11 + lax.dot_general(low, w, NT, precision=HI), -low], axis=1),
            jnp.concatenate([-low.T, inv22], axis=1),
        ],
        axis=0,
    )
    out[...] = 0.5 * inv + full(drive, inv)[0:1]


def update_kernel(weight, state, out):
    parts, rows, members, cols = state.shape
    x = patch_matrix(state)
    mean = jnp.sum(x, axis=0, keepdims=True) * (1.0 / (parts * members))
    anomaly = x - mean
    result = product3(weight[...], anomaly) + (mean + 0.5 * anomaly)
    for p in range(parts):
        for i in range(rows):
            out[p, i] = result[p * members : (p + 1) * members, i * cols : (i + 1) * cols]


VMEM = pl.BlockSpec(memory_space=pltpu.VMEM)
SMEM = pl.BlockSpec(memory_space=pltpu.SMEM)
PARAMS = pltpu.CompilerParams(vmem_limit_bytes=20 * 1024 * 1024)


def f32(*shape):
    return jax.ShapeDtypeStruct(shape, jnp.float32)


def paired(x, axis, first):
    n = lax.axis_size(axis)
    pairs = [(i, (i + 1) % n) for i in range(first, n, 2)]
    return lax.ppermute(x, axis, pairs + [(j, i) for i, j in pairs])


def swap(x):
    return lax.all_to_all(x, "member", split_axis=0, concat_axis=0, tiled=True)


def on_device(ensemble, speed_row, speed_col, obs_cell, obs_value, obs_var, obs_count, loc_slots):
    members, rows, width = ensemble.shape
    parts = lax.axis_size("member")
    cols = width // parts
    groups = members // SUB
    per_patch, obs = obs_cell.shape[3:]
    total = parts * members

    planes = ensemble.transpose(1, 0, 2)
    across, within = pl.pallas_call(
        edge_kernel,
        out_shape=(f32(2 * groups + 1, SUB, width), f32(2 * groups + 1, SUB, width)),
        in_specs=[pl.BlockSpec(memory_space=pltpu.HBM)] * 3,
        out_specs=(VMEM, VMEM),
        scratch_shapes=[
            pltpu.VMEM(ensemble.shape, jnp.float32),
            pltpu.VMEM(speed_row.shape, jnp.float32),
            pltpu.VMEM(speed_col.shape, jnp.float32),
            pltpu.SemaphoreType.DMA((groups + 2,)),
        ],
        compiler_params=pltpu.CompilerParams(vmem_limit_bytes=62 * 1024 * 1024),
        name="edges",
    )(ensemble, speed_row, speed_col)
    across = paired(across, "space", 1)
    within = paired(within, "space", 0)
    state = pl.pallas_call(
        advect_kernel,
        out_shape=f32(parts, rows, members, cols),
        in_specs=[VMEM] * 5,
        out_specs=VMEM,
        scratch_shapes=[pltpu.VMEM((rows + 2, 4, SUB, width), jnp.float32)],
        compiler_params=PARAMS,
        name="advect",
    )(planes, across, within, speed_row, speed_col)
    cell = swap(jnp.broadcast_to(obs_cell[0, 0], (parts, per_patch, obs)))
    raw = pl.pallas_call(
        gather_kernel,
        out_shape=f32(parts, per_patch, members, obs),
        in_specs=[VMEM] * 2,
        out_specs=VMEM,
        compiler_params=PARAMS,
        name="gather",
    )(state, cell)
    raw = swap(raw)
    tiles = pl.pallas_call(
        tile_kernel,
        out_shape=f32(per_patch, total + SUB, obs),
        in_specs=[SMEM] + [VMEM] * 3,
        out_specs=VMEM,
        compiler_params=PARAMS,
        name="tiles",
    )(obs_count[0, 0, 0], raw, obs_value[0, 0, 0], obs_var[0, 0, 0])
    within = paired(tiles, "space", 0)
    across = paired(tiles, "space", 1)
    even_z = paired(tiles, "member", 0)
    odd_z = paired(tiles, "member", 1)
    both_z = jnp.concatenate([even_z, odd_z])
    state = swap(state)
    within_c = paired(both_z, "space", 0)
    across_c = paired(both_z, "space", 1)
    slots = loc_slots[0, 0, 0]
    half = total // 2
    depth = per_patch * obs
    near = pl.pallas_call(
        functools.partial(near_kernel, per_patch),
        out_shape=(f32(half + SUB, half), f32(half + SUB, half), f32(half, half)),
        in_specs=[SMEM] + [VMEM] * 5,
        out_specs=(VMEM, VMEM, VMEM),
        scratch_shapes=[pltpu.VMEM((total + SUB, 5 * depth), jnp.float32)],
        compiler_params=PARAMS,
        cost_estimate=pl.CostEstimate(
            flops=240 * total * total * depth, bytes_accessed=12 * (total + SUB) * depth * 4, transcendentals=0
        ),
        name="near_gram",
    )(slots, tiles, odd_z, even_z, within, across)
    weight = pl.pallas_call(
        functools.partial(weight_kernel, per_patch),
        out_shape=f32(total, total),
        in_specs=[SMEM] + [VMEM] * 5,
        out_specs=VMEM,
        scratch_shapes=[pltpu.VMEM((total + SUB, 4 * depth), jnp.float32)],
        compiler_params=PARAMS,
        cost_estimate=pl.CostEstimate(
            flops=120 * total * total * depth, bytes_accessed=12 * total * total, transcendentals=0
        ),
        name="weights",
    )(slots, *near, within_c, across_c)
    state = pl.pallas_call(
        update_kernel,
        out_shape=f32(parts, rows, members, cols),
        in_specs=[VMEM] * 2,
        out_specs=VMEM,
        compiler_params=PARAMS,
        name="update",
    )(weight, state)
    state = swap(state)
    return state.transpose(2, 1, 0, 3).reshape(members, rows, width)


def solution(mesh):
    return jax.shard_map(
        on_device,
        mesh=mesh,
        in_specs=(
            P("member", "space", None),
            P("space", None),
            P("space", None),
            P("space", "member", None, None, None),
            P("space", "member", None, None, None),
            P("space", "member", None, None, None),
            P("space", "member", None, None),
            P("space", "member", None, None),
        ),
        out_specs=P("member", "space", None),
        check_vma=False,
    )
```

```python
import functools

import jax
import jax.numpy as jnp
from jax import lax
from jax.experimental import pallas as pl
from jax.experimental.pallas import tpu as pltpu
from jax.sharding import PartitionSpec as P

K = 0.2
HI = lax.Precision.HIGHEST
SUB = 8
NT = (((1,), (1,)), ((), ()))


def split3(x):
    a = x.astype(jnp.bfloat16)
    rest = x - a.astype(jnp.float32)
    b = rest.astype(jnp.bfloat16)
    c = (rest - b.astype(jnp.float32)).astype(jnp.bfloat16)
    return a, b, c


def split2(x):
    a = x.astype(jnp.bfloat16)
    return a, (x - a.astype(jnp.float32)).astype(jnp.bfloat16)


def product(a, b, dims=(((1,), (0,)), ((), ()))):
    (a, a_low), (b, b_low) = a, b
    dot = functools.partial(
        lax.dot_general, dimension_numbers=dims, preferred_element_type=jnp.float32
    )
    return dot(a, b) + (dot(a, b_low) + dot(a_low, b))


def product3(a, b):
    return product(split2(a), split2(b))


def full(a, b):
    return jnp.dot(a, b, precision=HI)


def eye(n):
    rows = lax.broadcasted_iota(jnp.int32, (n, n), 0)
    cols = lax.broadcasted_iota(jnp.int32, (n, n), 1)
    return jnp.where(rows == cols, 1.0, 0.0).astype(jnp.float32)


def parity(axis):
    return lax.rem(lax.axis_index(axis), 2)


def edge_kernel(ensemble_far, row_far, col_far, across, within, ensemble, speed_row, speed_col, done):
    members, rows, width = ensemble.shape
    groups = members // SUB
    odd = parity("space") == 1

    def fetch(far, near, n):
        return pltpu.make_async_copy(far, near, done.at[n])

    def part(g):
        at = pl.ds(g * SUB, SUB)
        return fetch(ensemble_far.at[at], ensemble.at[at], g)

    copies = [part(g) for g in range(groups)]
    copies += [fetch(row_far, speed_row, groups), fetch(col_far, speed_col, groups + 1)]
    for copy in copies:
        copy.start()

    def put(at, low, high):
        across[at] = jnp.where(odd, high, low)
        within[at] = jnp.where(odd, low, high)

    for g in range(groups):
        copies[g].wait()
        for n in range(2):
            low = ensemble[g * SUB : (g + 1) * SUB, n, :]
            high = ensemble[g * SUB : (g + 1) * SUB, rows - 2 + n, :]
            put(n * groups + g, low, high)
    across[2 * groups] = jnp.zeros((SUB, width), jnp.float32)
    within[2 * groups] = jnp.zeros((SUB, width), jnp.float32)
    for n, speed in enumerate((speed_row, speed_col)):
        copies[groups + n].wait()
        put((2 * groups, slice(n, n + 1)), speed[0:1], speed[rows - 1 : rows])


def advect_kernel(planes, across, within, speed_row, speed_col, out, far, coef, done):
    rows, members, width = planes.shape
    blocks = out.shape[0]
    cols = out.shape[3]
    groups = members // SUB
    odd = parity("space") == 1

    def before(at):
        return jnp.where(odd, within[at], across[at])

    def after(at):
        return jnp.where(odd, across[at], within[at])

    top, bottom = before(2 * groups), after(2 * groups)
    for r in range(rows + 2):
        if r == 0:
            u, v = top[0:1], top[1:2]
        elif r == rows + 1:
            u, v = bottom[0:1], bottom[1:2]
        else:
            u, v = speed_row[r - 1 : r], speed_col[r - 1 : r]
        for n, c in enumerate((K + 0.5 * u, K - 0.5 * u, K + 0.5 * v, K - 0.5 * v)):
            coef[r, n] = jnp.broadcast_to(c, (SUB, width))

    def step(field, first):
        new = []
        for n in range(1, len(field) - 1):
            r = first + n - 1
            x = field[n]
            new.append(
                (1.0 - 4.0 * K) * x
                + coef[r, 0] * field[n - 1]
                + coef[r, 1] * field[n + 1]
                + coef[r, 2] * pltpu.roll(x, 1, 1)
                + coef[r, 3] * pltpu.roll(x, width - 1, 1)
            )
        return new

    def body(g, carry):
        at = pl.ds(pl.multiple_of(g * SUB, SUB), SUB)
        field = [before(g), before(groups + g)]
        field += [planes[i, at, :] for i in range(rows)]
        field += [after(g), after(groups + g)]
        field = step(step(field, 0), 1)
        for i in range(rows):
            for b in range(blocks):
                out[b, i, at, :] = field[i][:, b * cols : (b + 1) * cols]
        store(g).start()
        return carry

    def store(g):
        at = pl.ds(pl.multiple_of(g * SUB, SUB), SUB)
        return pltpu.make_async_copy(out.at[:, :, at, :], far.at[:, :, at, :], done.at[g])

    lax.fori_loop(0, groups, body, 0)
    for g in range(groups):
        store(g).wait()


def patch_matrix(state):
    parts, rows, members, cols = state.shape
    return jnp.concatenate(
        [state[:, i].reshape(parts * members, cols) for i in range(rows)], axis=1
    )


def gather_kernel(state, cell, raw):
    blocks, rows, members, cols = state.shape
    per_patch, obs = cell.shape[1:]
    row = lax.broadcasted_iota(jnp.int32, (rows * cols, obs), 0)
    for b in range(blocks):
        x = jnp.concatenate([state[b, i] for i in range(rows)], axis=1)
        x = jnp.concatenate(split3(x)[::-1], axis=0)
        pick = [jnp.where(row == cell[b, t : t + 1, :], 1.0, 0.0) for t in range(per_patch)]
        pick = jnp.concatenate(pick, axis=1).astype(jnp.bfloat16)
        y = jnp.dot(x, pick, preferred_element_type=jnp.float32)
        y = y[:members] + y[members : 2 * members] + y[2 * members :]
        for t in range(per_patch):
            raw[b, t] = y[:, t * obs : (t + 1) * obs]


def tile_kernel(count, raw, value, variance, tiles):
    parts, per_patch, members, obs = raw.shape
    total = parts * members
    lane = lax.broadcasted_iota(jnp.int32, (1, obs), 1)
    below = lax.broadcasted_iota(jnp.int32, (SUB, obs), 0)
    for t in range(per_patch):
        y = raw[:, t].reshape(total, obs)
        mean = jnp.sum(y, axis=0, keepdims=True) * (1.0 / total)
        weight = jnp.where(lane < count[t], 1.0 / variance[t : t + 1, :], 0.0)
        scale = jnp.sqrt(weight * (1.0 / (total - 1.0)))
        tiles[t, 0:total, :] = (y - mean) * scale
        innovation = (value[t : t + 1, :] - mean) * scale
        tiles[t, total : total + SUB, :] = jnp.where(below == 0, innovation, 0.0)


def spd_inverse(s):
    n = s.shape[0]
    unit = eye(n)
    size = jnp.sum(s * s)
    bound = jnp.minimum(jnp.sqrt(size), jnp.max(jnp.sum(jnp.abs(s), axis=0)))
    bound = jnp.maximum(bound, 1.0) * 1.0001
    scale = 2.0 / (1.0 + bound)
    x = scale * unit
    e = unit - scale * s
    rho = (bound - 1.0) / (bound + 1.0)

    def quick_pair(x, e):
        e = split2(e)
        return product(split2(x), e), product(e, e)

    def full_pair(x, e):
        return full(x, e), full(e, e)

    def square(pair, carry):
        x, e, rho = carry
        x_more, e_more = pair(x, e)
        square_rho = rho * rho
        scale = 2.0 / (2.0 - square_rho)
        x = scale * (x + x_more)
        e = scale * e_more + (1.0 - scale) * unit
        return x, e, square_rho / (2.0 - square_rho)

    def quick(carry):
        return (carry[2] > 1e-3) & (bound < 1000.0)

    def careful(carry):
        return carry[2] > 1e-3

    carry = lax.while_loop(quick, functools.partial(square, quick_pair), (x, e, rho))
    x = lax.while_loop(careful, functools.partial(square, full_pair), carry)[0]

    def unsettled(carry):
        return (carry[1] > 1e-5) & (carry[2] < 8)

    def newton(carry):
        x, _, count = carry
        e = unit - full(s, x)
        return x + product3(x, e), jnp.sum(e * e), count + 1

    return lax.while_loop(unsettled, newton, (x, jnp.float32(1.0), jnp.int32(0)))[0]


def fill(z, slots, per_patch, tiles):
    odd_row, odd_col = parity("space"), parity("member")
    mask = jnp.int32(0)
    for n in range(slots.shape[0]):
        o, t = lax.div(slots[n], per_patch), lax.rem(slots[n], per_patch)
        r, s = lax.div(o, 3), lax.rem(o, 3)
        r = r + odd_row * (2 - 2 * r)
        s = s + odd_col * (2 - 2 * s)
        mask = mask | lax.shift_left(jnp.int32(1), (r * 3 + s) * per_patch + t)
    for n, (r, s, ref, first) in enumerate(tiles):
        for t in range(per_patch):
            bit = ((r + 1) * 3 + s + 1) * per_patch + t
            chosen = (lax.shift_right_logical(mask, bit) & 1).astype(jnp.float32)
            root = (1.0 / (1.0 + r * r + s * s)) ** 0.5
            obs = ref.shape[2]
            at = (n * per_patch + t) * obs
            z[:, at : at + obs] = ref[first + t] * (chosen * root)


def gram_blocks(z, total):
    half = total // 2
    z1, z2 = split2(z[0:half, :]), split2(z[half:total, :])
    zd = split2(z[total:, :])
    top = [jnp.concatenate([p, q], axis=0) for p, q in zip(z1, zd)]
    return product(top, z1, NT), product(top, z2, NT), product(z2, z2, NT)


def near_kernel(per_patch, slots, own, odd_z, even_z, within, across, gram1, gram2, gram3, z):
    tiles = ((0, 0, own, 0), (0, -1, odd_z, 0), (0, 1, even_z, 0), (-1, 0, across, 0), (1, 0, within, 0))
    fill(z, slots, per_patch, tiles)
    gram1[...], gram2[...], gram3[...] = gram_blocks(z, 2 * gram3.shape[0])


def weight_kernel(per_patch, slots, near1, near2, near3, within, across, out, z):
    half = near3.shape[0]
    total = 2 * half
    tiles = (
        (-1, 1, across, 0),
        (-1, -1, across, per_patch),
        (1, 1, within, 0),
        (1, -1, within, per_patch),
    )
    fill(z, slots, per_patch, tiles)
    gram1, gram2, gram3 = gram_blocks(z, total)
    gram1, gram2 = gram1 + near1[...], gram2 + near2[...]
    drive = jnp.concatenate([gram1[half:], gram2[half:]], axis=1)
    s11 = gram1[:half] + eye(half)
    s12 = gram2[:half]
    s22 = gram3 + near3[...] + eye(half)
    inv11 = spd_inverse(s11)
    w = jnp.dot(inv11, s12, precision=HI)
    schur = s22 - lax.dot_general(s12, w, (((0,), (0,)), ((), ())), precision=HI)
    inv22 = spd_inverse(0.5 * (schur + schur.T))
    low = jnp.dot(w, inv22, precision=HI)
    inv = jnp.concatenate(
        [
            jnp.concatenate([inv11 + lax.dot_general(low, w, NT, precision=HI), -low], axis=1),
            jnp.concatenate([-low.T, inv22], axis=1),
        ],
        axis=0,
    )
    out[...] = 0.5 * inv + full(drive, inv)[0:1]


def update_kernel(weight, state, out):
    parts, rows, members, cols = state.shape
    x = patch_matrix(state)
    mean = jnp.sum(x, axis=0, keepdims=True) * (1.0 / (parts * members))
    anomaly = x - mean
    result = product3(weight[...], anomaly) + (mean + 0.5 * anomaly)
    for p in range(parts):
        for i in range(rows):
            out[p, i] = result[p * members : (p + 1) * members, i * cols : (i + 1) * cols]


def output_kernel(state, out, near, done):
    blocks, rows, members, cols = state.shape
    step = members // done.shape[0]
    copies = []
    for g in range(done.shape[0]):
        at = pl.ds(g * step, step)
        for b in range(blocks):
            for i in range(rows):
                near[at, i, b * cols : (b + 1) * cols] = state[b, i, at]
        copies.append(pltpu.make_async_copy(near.at[at], out.at[at], done.at[g]))
        copies[-1].start()
    for copy in copies:
        copy.wait()


VMEM = pl.BlockSpec(memory_space=pltpu.VMEM)
HBM = pl.BlockSpec(memory_space=pltpu.HBM)
SMEM = pl.BlockSpec(memory_space=pltpu.SMEM)
PARAMS = pltpu.CompilerParams(vmem_limit_bytes=20 * 1024 * 1024)


def f32(*shape):
    return jax.ShapeDtypeStruct(shape, jnp.float32)


def paired(x, axis, first):
    n = lax.axis_size(axis)
    pairs = [(i, (i + 1) % n) for i in range(first, n, 2)]
    return lax.ppermute(x, axis, pairs + [(j, i) for i, j in pairs])


def swap(x):
    return lax.all_to_all(x, "member", split_axis=0, concat_axis=0, tiled=True)


def on_device(ensemble, speed_row, speed_col, obs_cell, obs_value, obs_var, obs_count, loc_slots):
    members, rows, width = ensemble.shape
    parts = lax.axis_size("member")
    cols = width // parts
    groups = members // SUB
    per_patch, obs = obs_cell.shape[3:]
    total = parts * members

    planes = ensemble.transpose(1, 0, 2)
    across, within = pl.pallas_call(
        edge_kernel,
        out_shape=(f32(2 * groups + 1, SUB, width), f32(2 * groups + 1, SUB, width)),
        in_specs=[HBM] * 3,
        out_specs=(VMEM, VMEM),
        scratch_shapes=[
            pltpu.VMEM(ensemble.shape, jnp.float32),
            pltpu.VMEM(speed_row.shape, jnp.float32),
            pltpu.VMEM(speed_col.shape, jnp.float32),
            pltpu.SemaphoreType.DMA((groups + 2,)),
        ],
        compiler_params=pltpu.CompilerParams(vmem_limit_bytes=62 * 1024 * 1024),
        name="edges",
    )(ensemble, speed_row, speed_col)
    across = paired(across, "space", 1)
    within = paired(within, "space", 0)
    fresh, state = pl.pallas_call(
        advect_kernel,
        out_shape=(f32(parts, rows, members, cols), f32(parts, rows, members, cols)),
        in_specs=[VMEM] * 5,
        out_specs=(VMEM, HBM),
        scratch_shapes=[
            pltpu.VMEM((rows + 2, 4, SUB, width), jnp.float32),
            pltpu.SemaphoreType.DMA((groups,)),
        ],
        compiler_params=PARAMS,
        name="advect",
    )(planes, across, within, speed_row, speed_col)
    cell = swap(jnp.broadcast_to(obs_cell[0, 0], (parts, per_patch, obs)))
    raw = pl.pallas_call(
        gather_kernel,
        out_shape=f32(parts, per_patch, members, obs),
        in_specs=[VMEM] * 2,
        out_specs=VMEM,
        compiler_params=PARAMS,
        name="gather",
    )(fresh, cell)
    raw = swap(raw)
    tiles = pl.pallas_call(
        tile_kernel,
        out_shape=f32(per_patch, total + SUB, obs),
        in_specs=[SMEM] + [VMEM] * 3,
        out_specs=VMEM,
        compiler_params=PARAMS,
        name="tiles",
    )(obs_count[0, 0, 0], raw, obs_value[0, 0, 0], obs_var[0, 0, 0])
    within = paired(tiles, "space", 0)
    across = paired(tiles, "space", 1)
    even_z = paired(tiles, "member", 0)
    odd_z = paired(tiles, "member", 1)
    both_z = jnp.concatenate([even_z, odd_z])
    state = swap(state)
    within_c = paired(both_z, "space", 0)
    across_c = paired(both_z, "space", 1)
    slots = loc_slots[0, 0, 0]
    half = total // 2
    depth = per_patch * obs
    near = pl.pallas_call(
        functools.partial(near_kernel, per_patch),
        out_shape=(f32(half + SUB, half), f32(half + SUB, half), f32(half, half)),
        in_specs=[SMEM] + [VMEM] * 5,
        out_specs=(VMEM, VMEM, VMEM),
        scratch_shapes=[pltpu.VMEM((total + SUB, 5 * depth), jnp.float32)],
        compiler_params=PARAMS,
        cost_estimate=pl.CostEstimate(
            flops=240 * total * total * depth, bytes_accessed=12 * (total + SUB) * depth * 4, transcendentals=0
        ),
        name="near_gram",
    )(slots, tiles, odd_z, even_z, within, across)
    weight = pl.pallas_call(
        functools.partial(weight_kernel, per_patch),
        out_shape=f32(total, total),
        in_specs=[SMEM] + [VMEM] * 5,
        out_specs=VMEM,
        scratch_shapes=[pltpu.VMEM((total + SUB, 4 * depth), jnp.float32)],
        compiler_params=PARAMS,
        cost_estimate=pl.CostEstimate(
            flops=120 * total * total * depth, bytes_accessed=12 * total * total, transcendentals=0
        ),
        name="weights",
    )(slots, *near, within_c, across_c)
    state = pl.pallas_call(
        update_kernel,
        out_shape=f32(parts, rows, members, cols),
        in_specs=[VMEM] * 2,
        out_specs=VMEM,
        compiler_params=PARAMS,
        name="update",
    )(weight, state)
    state = swap(state)
    return pl.pallas_call(
        output_kernel,
        out_shape=f32(members, rows, width),
        in_specs=[VMEM],
        out_specs=HBM,
        scratch_shapes=[
            pltpu.VMEM((members, rows, width), jnp.float32),
            pltpu.SemaphoreType.DMA((4,)),
        ],
        compiler_params=PARAMS,
        name="output",
    )(state)


def solution(mesh):
    return jax.shard_map(
        on_device,
        mesh=mesh,
        in_specs=(
            P("member", "space", None),
            P("space", None),
            P("space", None),
            P("space", "member", None, None, None),
            P("space", "member", None, None, None),
            P("space", "member", None, None, None),
            P("space", "member", None, None),
            P("space", "member", None, None),
        ),
        out_specs=P("member", "space", None),
        check_vma=False,
    )
```

```python
import functools

import jax
import jax.numpy as jnp
from jax import lax
from jax.experimental import pallas as pl
from jax.experimental.pallas import tpu as pltpu
from jax.sharding import PartitionSpec as P

K = 0.2
HI = lax.Precision.HIGHEST
SUB = 8
NT = (((1,), (1,)), ((), ()))


def split3(x):
    a = x.astype(jnp.bfloat16)
    rest = x - a.astype(jnp.float32)
    b = rest.astype(jnp.bfloat16)
    c = (rest - b.astype(jnp.float32)).astype(jnp.bfloat16)
    return a, b, c


def split2(x):
    a = x.astype(jnp.bfloat16)
    return a, (x - a.astype(jnp.float32)).astype(jnp.bfloat16)


def product(a, b, dims=(((1,), (0,)), ((), ()))):
    (a, a_low), (b, b_low) = a, b
    dot = functools.partial(
        lax.dot_general, dimension_numbers=dims, preferred_element_type=jnp.float32
    )
    return dot(a, b) + (dot(a, b_low) + dot(a_low, b))


def product3(a, b):
    return product(split2(a), split2(b))


def full(a, b):
    return jnp.dot(a, b, precision=HI)


def eye(n):
    rows = lax.broadcasted_iota(jnp.int32, (n, n), 0)
    cols = lax.broadcasted_iota(jnp.int32, (n, n), 1)
    return jnp.where(rows == cols, 1.0, 0.0).astype(jnp.float32)


def parity(axis):
    return lax.rem(lax.axis_index(axis), 2)


def edge_kernel(ensemble_far, row_far, col_far, across, within, ensemble, speed_row, speed_col, done):
    members, rows, width = ensemble.shape
    groups = members // SUB
    odd = parity("space") == 1

    def fetch(far, near, n):
        return pltpu.make_async_copy(far, near, done.at[n])

    def part(g):
        at = pl.ds(g * SUB, SUB)
        return fetch(ensemble_far.at[at], ensemble.at[at], g)

    copies = [part(g) for g in range(groups)]
    copies += [fetch(row_far, speed_row, groups), fetch(col_far, speed_col, groups + 1)]
    for copy in copies:
        copy.start()

    def put(at, low, high):
        across[at] = jnp.where(odd, high, low)
        within[at] = jnp.where(odd, low, high)

    for g in range(groups):
        copies[g].wait()
        for n in range(2):
            low = ensemble[g * SUB : (g + 1) * SUB, n, :]
            high = ensemble[g * SUB : (g + 1) * SUB, rows - 2 + n, :]
            put(n * groups + g, low, high)
    across[2 * groups] = jnp.zeros((SUB, width), jnp.float32)
    within[2 * groups] = jnp.zeros((SUB, width), jnp.float32)
    for n, speed in enumerate((speed_row, speed_col)):
        copies[groups + n].wait()
        put((2 * groups, slice(n, n + 1)), speed[0:1], speed[rows - 1 : rows])


def advect_kernel(planes, across, within, speed_row, speed_col, out, far, coef, done):
    rows, members, width = planes.shape
    blocks = out.shape[0]
    cols = out.shape[3]
    groups = members // SUB
    odd = parity("space") == 1

    def before(at):
        return jnp.where(odd, within[at], across[at])

    def after(at):
        return jnp.where(odd, across[at], within[at])

    top, bottom = before(2 * groups), after(2 * groups)
    for r in range(rows + 2):
        if r == 0:
            u, v = top[0:1], top[1:2]
        elif r == rows + 1:
            u, v = bottom[0:1], bottom[1:2]
        else:
            u, v = speed_row[r - 1 : r], speed_col[r - 1 : r]
        for n, c in enumerate((K + 0.5 * u, K - 0.5 * u, K + 0.5 * v, K - 0.5 * v)):
            coef[r, n] = jnp.broadcast_to(c, (SUB, width))

    def step(field, first):
        new = []
        for n in range(1, len(field) - 1):
            r = first + n - 1
            x = field[n]
            new.append(
                (1.0 - 4.0 * K) * x
                + coef[r, 0] * field[n - 1]
                + coef[r, 1] * field[n + 1]
                + coef[r, 2] * pltpu.roll(x, 1, 1)
                + coef[r, 3] * pltpu.roll(x, width - 1, 1)
            )
        return new

    def body(g, carry):
        at = pl.ds(pl.multiple_of(g * SUB, SUB), SUB)
        field = [before(g), before(groups + g)]
        field += [planes[i, at, :] for i in range(rows)]
        field += [after(g), after(groups + g)]
        field = step(step(field, 0), 1)
        for i in range(rows):
            for b in range(blocks):
                out[b, i, at, :] = field[i][:, b * cols : (b + 1) * cols]
        store(g).start()
        return carry

    def store(g):
        at = pl.ds(pl.multiple_of(g * SUB, SUB), SUB)
        return pltpu.make_async_copy(out.at[:, :, at, :], far.at[:, :, at, :], done.at[g])

    lax.fori_loop(0, groups, body, 0)
    for g in range(groups):
        store(g).wait()


def patch_matrix(state):
    parts, rows, members, cols = state.shape
    return jnp.concatenate(
        [state[:, i].reshape(parts * members, cols) for i in range(rows)], axis=1
    )


def gather_kernel(state, cell, raw):
    blocks, rows, members, cols = state.shape
    per_patch, obs = cell.shape[1:]
    row = lax.broadcasted_iota(jnp.int32, (rows * cols, obs), 0)
    for b in range(blocks):
        x = jnp.concatenate([state[b, i] for i in range(rows)], axis=1)
        x = jnp.concatenate(split3(x)[::-1], axis=0)
        pick = [jnp.where(row == cell[b, t : t + 1, :], 1.0, 0.0) for t in range(per_patch)]
        pick = jnp.concatenate(pick, axis=1).astype(jnp.bfloat16)
        y = jnp.dot(x, pick, preferred_element_type=jnp.float32)
        y = y[:members] + y[members : 2 * members] + y[2 * members :]
        for t in range(per_patch):
            raw[b, t] = y[:, t * obs : (t + 1) * obs]


def tile_kernel(count, raw, value, variance, tiles):
    parts, per_patch, members, obs = raw.shape
    total = parts * members
    lane = lax.broadcasted_iota(jnp.int32, (1, obs), 1)
    below = lax.broadcasted_iota(jnp.int32, (SUB, obs), 0)
    for t in range(per_patch):
        y = raw[:, t].reshape(total, obs)
        mean = jnp.sum(y, axis=0, keepdims=True) * (1.0 / total)
        weight = jnp.where(lane < count[t], 1.0 / variance[t : t + 1, :], 0.0)
        scale = jnp.sqrt(weight * (1.0 / (total - 1.0)))
        tiles[t, 0:total, :] = (y - mean) * scale
        innovation = (value[t : t + 1, :] - mean) * scale
        tiles[t, total : total + SUB, :] = jnp.where(below == 0, innovation, 0.0)


def spd_inverse(s):
    n = s.shape[0]
    unit = eye(n)
    size = jnp.sum(s * s)
    bound = jnp.minimum(jnp.sqrt(size), jnp.max(jnp.sum(jnp.abs(s), axis=0)))
    bound = jnp.maximum(bound, 1.0) * 1.0001
    scale = 2.0 / (1.0 + bound)
    x = scale * unit
    e = unit - scale * s
    rho = (bound - 1.0) / (bound + 1.0)

    def quick_pair(x, e):
        e = split2(e)
        return product(split2(x), e), product(e, e)

    def full_pair(x, e):
        return full(x, e), full(e, e)

    def square(pair, carry):
        x, e, rho = carry
        x_more, e_more = pair(x, e)
        square_rho = rho * rho
        scale = 2.0 / (2.0 - square_rho)
        x = scale * (x + x_more)
        e = scale * e_more + (1.0 - scale) * unit
        return x, e, square_rho / (2.0 - square_rho)

    def quick(carry):
        return (carry[2] > 2e-4) & (bound < 1000.0)

    def careful(carry):
        return carry[2] > 2e-4

    carry = lax.while_loop(quick, functools.partial(square, quick_pair), (x, e, rho))
    x = lax.while_loop(careful, functools.partial(square, full_pair), carry)[0]

    def unsettled(carry):
        return (carry[1] > 1e-5) & (carry[2] < 8)

    def newton(carry):
        x, _, count = carry
        e = unit - full(s, x)
        return x + product3(x, e), jnp.sum(e * e), count + 1

    return lax.while_loop(unsettled, newton, (x, jnp.float32(1.0), jnp.int32(0)))[0]


def fill(z, slots, per_patch, tiles):
    odd_row, odd_col = parity("space"), parity("member")
    mask = jnp.int32(0)
    for n in range(slots.shape[0]):
        o, t = lax.div(slots[n], per_patch), lax.rem(slots[n], per_patch)
        r, s = lax.div(o, 3), lax.rem(o, 3)
        r = r + odd_row * (2 - 2 * r)
        s = s + odd_col * (2 - 2 * s)
        mask = mask | lax.shift_left(jnp.int32(1), (r * 3 + s) * per_patch + t)
    for n, (r, s, ref, first) in enumerate(tiles):
        for t in range(per_patch):
            bit = ((r + 1) * 3 + s + 1) * per_patch + t
            chosen = (lax.shift_right_logical(mask, bit) & 1).astype(jnp.float32)
            root = (1.0 / (1.0 + r * r + s * s)) ** 0.5
            obs = ref.shape[2]
            at = (n * per_patch + t) * obs
            z[:, at : at + obs] = ref[first + t] * (chosen * root)


def gram_blocks(z, total):
    half = total // 2
    z1, z2 = split2(z[0:half, :]), split2(z[half:total, :])
    zd = split2(z[total:, :])
    top = [jnp.concatenate([p, q], axis=0) for p, q in zip(z1, zd)]
    return product(top, z1, NT), product(top, z2, NT), product(z2, z2, NT)


def near_kernel(per_patch, slots, own, odd_z, even_z, across, within, gram1, gram2, gram3, z):
    tiles = ((0, 0, own, 0), (0, -1, odd_z, 0), (0, 1, even_z, 0), (-1, 0, across, 0), (1, 0, within, 0))
    fill(z, slots, per_patch, tiles)
    gram1[...], gram2[...], gram3[...] = gram_blocks(z, 2 * gram3.shape[0])


def corner_kernel(per_patch, slots, near1, near2, near3, within, gram1, gram2, gram3, z):
    fill(z, slots, per_patch, ((1, 1, within, 0), (1, -1, within, per_patch)))
    more1, more2, more3 = gram_blocks(z, 2 * near3.shape[0])
    gram1[...] = near1[...] + more1
    gram2[...] = near2[...] + more2
    gram3[...] = near3[...] + more3


def weight_kernel(per_patch, slots, near1, near2, near3, across, out, z):
    half = near3.shape[0]
    total = 2 * half
    tiles = (
        (-1, 1, across, 0),
        (-1, -1, across, per_patch),
    )
    fill(z, slots, per_patch, tiles)
    gram1, gram2, gram3 = gram_blocks(z, total)
    gram1, gram2 = gram1 + near1[...], gram2 + near2[...]
    drive = jnp.concatenate([gram1[half:], gram2[half:]], axis=1)
    s11 = gram1[:half] + eye(half)
    s12 = gram2[:half]
    s22 = gram3 + near3[...] + eye(half)
    inv11 = spd_inverse(s11)
    w = jnp.dot(inv11, s12, precision=HI)
    schur = s22 - lax.dot_general(s12, w, (((0,), (0,)), ((), ())), precision=HI)
    inv22 = spd_inverse(0.5 * (schur + schur.T))
    low = jnp.dot(w, inv22, precision=HI)
    inv = jnp.concatenate(
        [
            jnp.concatenate([inv11 + lax.dot_general(low, w, NT, precision=HI), -low], axis=1),
            jnp.concatenate([-low.T, inv22], axis=1),
        ],
        axis=0,
    )
    out[...] = 0.5 * inv + full(drive, inv)[0:1]


def update_kernel(weight, state, out):
    parts, rows, members, cols = state.shape
    x = patch_matrix(state)
    mean = jnp.sum(x, axis=0, keepdims=True) * (1.0 / (parts * members))
    anomaly = x - mean
    result = product3(weight[...], anomaly) + (mean + 0.5 * anomaly)
    for p in range(parts):
        for i in range(rows):
            out[p, i] = result[p * members : (p + 1) * members, i * cols : (i + 1) * cols]


def output_kernel(state, out, near, done):
    blocks, rows, members, cols = state.shape
    step = members // done.shape[0]
    copies = []
    for g in range(done.shape[0]):
        at = pl.ds(g * step, step)
        for b in range(blocks):
            for i in range(rows):
                near[at, i, b * cols : (b + 1) * cols] = state[b, i, at]
        copies.append(pltpu.make_async_copy(near.at[at], out.at[at], done.at[g]))
        copies[-1].start()
    for copy in copies:
        copy.wait()


VMEM = pl.BlockSpec(memory_space=pltpu.VMEM)
HBM = pl.BlockSpec(memory_space=pltpu.HBM)
SMEM = pl.BlockSpec(memory_space=pltpu.SMEM)
PARAMS = pltpu.CompilerParams(vmem_limit_bytes=20 * 1024 * 1024)


def f32(*shape):
    return jax.ShapeDtypeStruct(shape, jnp.float32)


def paired(x, axis, first):
    n = lax.axis_size(axis)
    pairs = [(i, (i + 1) % n) for i in range(first, n, 2)]
    return lax.ppermute(x, axis, pairs + [(j, i) for i, j in pairs])


def swap(x):
    return lax.all_to_all(x, "member", split_axis=0, concat_axis=0, tiled=True)


def on_device(ensemble, speed_row, speed_col, obs_cell, obs_value, obs_var, obs_count, loc_slots):
    members, rows, width = ensemble.shape
    parts = lax.axis_size("member")
    cols = width // parts
    groups = members // SUB
    per_patch, obs = obs_cell.shape[3:]
    total = parts * members

    planes = ensemble.transpose(1, 0, 2)
    across, within = pl.pallas_call(
        edge_kernel,
        out_shape=(f32(2 * groups + 1, SUB, width), f32(2 * groups + 1, SUB, width)),
        in_specs=[HBM] * 3,
        out_specs=(VMEM, VMEM),
        scratch_shapes=[
            pltpu.VMEM(ensemble.shape, jnp.float32),
            pltpu.VMEM(speed_row.shape, jnp.float32),
            pltpu.VMEM(speed_col.shape, jnp.float32),
            pltpu.SemaphoreType.DMA((groups + 2,)),
        ],
        compiler_params=pltpu.CompilerParams(vmem_limit_bytes=62 * 1024 * 1024),
        name="edges",
    )(ensemble, speed_row, speed_col)
    across = paired(across, "space", 1)
    within = paired(within, "space", 0)
    fresh, state = pl.pallas_call(
        advect_kernel,
        out_shape=(f32(parts, rows, members, cols), f32(parts, rows, members, cols)),
        in_specs=[VMEM] * 5,
        out_specs=(VMEM, HBM),
        scratch_shapes=[
            pltpu.VMEM((rows + 2, 4, SUB, width), jnp.float32),
            pltpu.SemaphoreType.DMA((groups,)),
        ],
        compiler_params=PARAMS,
        name="advect",
    )(planes, across, within, speed_row, speed_col)
    cell = swap(jnp.broadcast_to(obs_cell[0, 0], (parts, per_patch, obs)))
    raw = pl.pallas_call(
        gather_kernel,
        out_shape=f32(parts, per_patch, members, obs),
        in_specs=[VMEM] * 2,
        out_specs=VMEM,
        compiler_params=PARAMS,
        name="gather",
    )(fresh, cell)
    raw = swap(raw)
    tiles = pl.pallas_call(
        tile_kernel,
        out_shape=f32(per_patch, total + SUB, obs),
        in_specs=[SMEM] + [VMEM] * 3,
        out_specs=VMEM,
        compiler_params=PARAMS,
        name="tiles",
    )(obs_count[0, 0, 0], raw, obs_value[0, 0, 0], obs_var[0, 0, 0])
    within = paired(tiles, "space", 0)
    across = paired(tiles, "space", 1)
    even_z = paired(tiles, "member", 0)
    odd_z = paired(tiles, "member", 1)
    both_z = jnp.concatenate([even_z, odd_z])
    state = swap(state)
    late_z, across, within = lax.optimization_barrier((both_z, across, within))
    within_c = paired(late_z, "space", 0)
    across_c = paired(both_z, "space", 1)
    slots = loc_slots[0, 0, 0]
    half = total // 2
    depth = per_patch * obs
    near = pl.pallas_call(
        functools.partial(near_kernel, per_patch),
        out_shape=(f32(half + SUB, half), f32(half + SUB, half), f32(half, half)),
        in_specs=[SMEM] + [VMEM] * 5,
        out_specs=(VMEM, VMEM, VMEM),
        scratch_shapes=[pltpu.VMEM((total + SUB, 5 * depth), jnp.float32)],
        compiler_params=PARAMS,
        cost_estimate=pl.CostEstimate(
            flops=240 * total * total * depth, bytes_accessed=12 * (total + SUB) * depth * 4, transcendentals=0
        ),
        name="near_gram",
    )(slots, tiles, odd_z, even_z, across, within)
    near = pl.pallas_call(
        functools.partial(corner_kernel, per_patch),
        out_shape=(f32(half + SUB, half), f32(half + SUB, half), f32(half, half)),
        in_specs=[SMEM] + [VMEM] * 4,
        out_specs=(VMEM, VMEM, VMEM),
        scratch_shapes=[pltpu.VMEM((total + SUB, 2 * depth), jnp.float32)],
        compiler_params=PARAMS,
        cost_estimate=pl.CostEstimate(
            flops=6 * total * total * depth, bytes_accessed=12 * total * total, transcendentals=0
        ),
        name="corner_gram",
    )(slots, *near, within_c)
    weight = pl.pallas_call(
        functools.partial(weight_kernel, per_patch),
        out_shape=f32(total, total),
        in_specs=[SMEM] + [VMEM] * 4,
        out_specs=VMEM,
        scratch_shapes=[pltpu.VMEM((total + SUB, 2 * depth), jnp.float32)],
        compiler_params=PARAMS,
        cost_estimate=pl.CostEstimate(
            flops=120 * total * total * depth, bytes_accessed=12 * total * total, transcendentals=0
        ),
        name="weights",
    )(slots, *near, across_c)
    state = pl.pallas_call(
        update_kernel,
        out_shape=f32(parts, rows, members, cols),
        in_specs=[VMEM] * 2,
        out_specs=VMEM,
        compiler_params=PARAMS,
        name="update",
    )(weight, state)
    state = swap(state)
    return pl.pallas_call(
        output_kernel,
        out_shape=f32(members, rows, width),
        in_specs=[VMEM],
        out_specs=HBM,
        scratch_shapes=[
            pltpu.VMEM((members, rows, width), jnp.float32),
            pltpu.SemaphoreType.DMA((4,)),
        ],
        compiler_params=PARAMS,
        name="output",
    )(state)


def solution(mesh):
    return jax.shard_map(
        on_device,
        mesh=mesh,
        in_specs=(
            P("member", "space", None),
            P("space", None),
            P("space", None),
            P("space", "member", None, None, None),
            P("space", "member", None, None, None),
            P("space", "member", None, None, None),
            P("space", "member", None, None),
            P("space", "member", None, None),
        ),
        out_specs=P("member", "space", None),
        check_vma=False,
    )
```

```python
import functools

import jax
import jax.numpy as jnp
from jax import lax
from jax.experimental import pallas as pl
from jax.experimental.pallas import tpu as pltpu
from jax.sharding import PartitionSpec as P

K = 0.2
HI = lax.Precision.HIGHEST
SUB = 8
NT = (((1,), (1,)), ((), ()))


def split3(x):
    a = x.astype(jnp.bfloat16)
    rest = x - a.astype(jnp.float32)
    b = rest.astype(jnp.bfloat16)
    c = (rest - b.astype(jnp.float32)).astype(jnp.bfloat16)
    return a, b, c


def split2(x):
    a = x.astype(jnp.bfloat16)
    return a, (x - a.astype(jnp.float32)).astype(jnp.bfloat16)


def product(a, b, dims=(((1,), (0,)), ((), ()))):
    (a, a_low), (b, b_low) = a, b
    dot = functools.partial(
        lax.dot_general, dimension_numbers=dims, preferred_element_type=jnp.float32
    )
    return dot(a, b) + (dot(a, b_low) + dot(a_low, b))


def product3(a, b):
    return product(split2(a), split2(b))


def full(a, b):
    return jnp.dot(a, b, precision=HI)


def eye(n):
    rows = lax.broadcasted_iota(jnp.int32, (n, n), 0)
    cols = lax.broadcasted_iota(jnp.int32, (n, n), 1)
    return jnp.where(rows == cols, 1.0, 0.0).astype(jnp.float32)


def parity(axis):
    return lax.rem(lax.axis_index(axis), 2)


def edge_kernel(
    ensemble_far, row_far, col_far, cell_far, across, within, cells, ensemble, speed_row, speed_col, cell, done
):
    members, rows, width = ensemble.shape
    groups = members // SUB
    odd = parity("space") == 1

    def fetch(far, near, n):
        return pltpu.make_async_copy(far, near, done.at[n])

    def part(g):
        at = pl.ds(g * SUB, SUB)
        return fetch(ensemble_far.at[at], ensemble.at[at], g)

    copies = [part(g) for g in range(groups)]
    copies += [fetch(row_far, speed_row, groups), fetch(col_far, speed_col, groups + 1)]
    copies += [fetch(cell_far, cell, groups + 2)]
    for copy in copies:
        copy.start()

    def put(at, low, high):
        across[at] = jnp.where(odd, high, low)
        within[at] = jnp.where(odd, low, high)

    for g in range(groups):
        copies[g].wait()
        for n in range(2):
            low = ensemble[g * SUB : (g + 1) * SUB, n, :]
            high = ensemble[g * SUB : (g + 1) * SUB, rows - 2 + n, :]
            put(n * groups + g, low, high)
    across[2 * groups] = jnp.zeros((SUB, width), jnp.float32)
    within[2 * groups] = jnp.zeros((SUB, width), jnp.float32)
    for n, speed in enumerate((speed_row, speed_col)):
        copies[groups + n].wait()
        put((2 * groups, slice(n, n + 1)), speed[0:1], speed[rows - 1 : rows])
    copies[groups + 2].wait()
    for b in range(cells.shape[0]):
        cells[b] = cell[...]


def advect_kernel(planes, across, within, speed_row, speed_col, out, far, coef, done):
    rows, members, width = planes.shape
    blocks = out.shape[0]
    cols = out.shape[3]
    groups = members // SUB
    odd = parity("space") == 1

    def before(at):
        return jnp.where(odd, within[at], across[at])

    def after(at):
        return jnp.where(odd, across[at], within[at])

    top, bottom = before(2 * groups), after(2 * groups)
    for r in range(rows + 2):
        if r == 0:
            u, v = top[0:1], top[1:2]
        elif r == rows + 1:
            u, v = bottom[0:1], bottom[1:2]
        else:
            u, v = speed_row[r - 1 : r], speed_col[r - 1 : r]
        for n, c in enumerate((K + 0.5 * u, K - 0.5 * u, K + 0.5 * v, K - 0.5 * v)):
            coef[r, n] = jnp.broadcast_to(c, (SUB, width))

    def step(field, first):
        new = []
        for n in range(1, len(field) - 1):
            r = first + n - 1
            x = field[n]
            new.append(
                (1.0 - 4.0 * K) * x
                + coef[r, 0] * field[n - 1]
                + coef[r, 1] * field[n + 1]
                + coef[r, 2] * pltpu.roll(x, 1, 1)
                + coef[r, 3] * pltpu.roll(x, width - 1, 1)
            )
        return new

    def body(g, carry):
        at = pl.ds(pl.multiple_of(g * SUB, SUB), SUB)
        field = [before(g), before(groups + g)]
        field += [planes[i, at, :] for i in range(rows)]
        field += [after(g), after(groups + g)]
        field = step(step(field, 0), 1)
        for i in range(rows):
            for b in range(blocks):
                out[b, i, at, :] = field[i][:, b * cols : (b + 1) * cols]
        store(g).start()
        return carry

    def store(g):
        at = pl.ds(pl.multiple_of(g * SUB, SUB), SUB)
        return pltpu.make_async_copy(out.at[:, :, at, :], far.at[:, :, at, :], done.at[g])

    lax.fori_loop(0, groups, body, 0)
    for g in range(groups):
        store(g).wait()


def patch_matrix(state):
    parts, rows, members, cols = state.shape
    return jnp.concatenate(
        [state[:, i].reshape(parts * members, cols) for i in range(rows)], axis=1
    )


def gather_kernel(state, cell, raw):
    blocks, rows, members, cols = state.shape
    per_patch, obs = cell.shape[1:]
    row = lax.broadcasted_iota(jnp.int32, (rows * cols, obs), 0)
    for b in range(blocks):
        x = jnp.concatenate([state[b, i] for i in range(rows)], axis=1)
        x = jnp.concatenate(split3(x)[::-1], axis=0)
        pick = [jnp.where(row == cell[b, t : t + 1, :], 1.0, 0.0) for t in range(per_patch)]
        pick = jnp.concatenate(pick, axis=1).astype(jnp.bfloat16)
        y = jnp.dot(x, pick, preferred_element_type=jnp.float32)
        y = y[:members] + y[members : 2 * members] + y[2 * members :]
        for t in range(per_patch):
            raw[b, t] = y[:, t * obs : (t + 1) * obs]


def tile_kernel(count, raw, value, variance, tiles):
    parts, per_patch, members, obs = raw.shape
    total = parts * members
    lane = lax.broadcasted_iota(jnp.int32, (1, obs), 1)
    below = lax.broadcasted_iota(jnp.int32, (SUB, obs), 0)
    for t in range(per_patch):
        y = raw[:, t].reshape(total, obs)
        mean = jnp.sum(y, axis=0, keepdims=True) * (1.0 / total)
        weight = jnp.where(lane < count[t], 1.0 / variance[t : t + 1, :], 0.0)
        scale = jnp.sqrt(weight * (1.0 / (total - 1.0)))
        tiles[t, 0:total, :] = (y - mean) * scale
        innovation = (value[t : t + 1, :] - mean) * scale
        tiles[t, total : total + SUB, :] = jnp.where(below == 0, innovation, 0.0)


def spd_inverse(s):
    n = s.shape[0]
    unit = eye(n)
    size = jnp.sum(s * s)
    bound = jnp.minimum(jnp.sqrt(size), jnp.max(jnp.sum(jnp.abs(s), axis=0)))
    bound = jnp.maximum(bound, 1.0) * 1.0001
    scale = 2.0 / (1.0 + bound)
    x = scale * unit
    e = unit - scale * s
    rho = (bound - 1.0) / (bound + 1.0)

    def quick_pair(x, e):
        e = split2(e)
        return product(split2(x), e), product(e, e)

    def full_pair(x, e):
        return full(x, e), full(e, e)

    def square(pair, carry):
        x, e, rho = carry
        x_more, e_more = pair(x, e)
        square_rho = rho * rho
        scale = 2.0 / (2.0 - square_rho)
        x = scale * (x + x_more)
        e = scale * e_more + (1.0 - scale) * unit
        return x, e, square_rho / (2.0 - square_rho)

    def quick(carry):
        return (carry[2] > 2e-4) & (bound < 1000.0)

    def careful(carry):
        return carry[2] > 2e-4

    carry = lax.while_loop(quick, functools.partial(square, quick_pair), (x, e, rho))
    x = lax.while_loop(careful, functools.partial(square, full_pair), carry)[0]

    def unsettled(carry):
        return (carry[1] > 1e-5) & (carry[2] < 8)

    def newton(carry):
        x, _, count = carry
        e = unit - full(s, x)
        return x + product3(x, e), jnp.sum(e * e), count + 1

    return lax.while_loop(unsettled, newton, (x, jnp.float32(1.0), jnp.int32(0)))[0]


def fill(z, slots, per_patch, tiles):
    odd_row, odd_col = parity("space"), parity("member")
    mask = jnp.int32(0)
    for n in range(slots.shape[0]):
        o, t = lax.div(slots[n], per_patch), lax.rem(slots[n], per_patch)
        r, s = lax.div(o, 3), lax.rem(o, 3)
        r = r + odd_row * (2 - 2 * r)
        s = s + odd_col * (2 - 2 * s)
        mask = mask | lax.shift_left(jnp.int32(1), (r * 3 + s) * per_patch + t)
    for n, (r, s, ref, first) in enumerate(tiles):
        for t in range(per_patch):
            bit = ((r + 1) * 3 + s + 1) * per_patch + t
            chosen = (lax.shift_right_logical(mask, bit) & 1).astype(jnp.float32)
            root = (1.0 / (1.0 + r * r + s * s)) ** 0.5
            obs = ref.shape[2]
            at = (n * per_patch + t) * obs
            z[:, at : at + obs] = ref[first + t] * (chosen * root)


def gram_blocks(z, total):
    half = total // 2
    z1, z2 = split2(z[0:half, :]), split2(z[half:total, :])
    zd = split2(z[total:, :])
    top = [jnp.concatenate([p, q], axis=0) for p, q in zip(z1, zd)]
    return product(top, z1, NT), product(top, z2, NT), product(z2, z2, NT)


def near_kernel(per_patch, slots, own, odd_z, even_z, across, within, gram1, gram2, gram3, z):
    tiles = ((0, 0, own, 0), (0, -1, odd_z, 0), (0, 1, even_z, 0), (-1, 0, across, 0), (1, 0, within, 0))
    fill(z, slots, per_patch, tiles)
    gram1[...], gram2[...], gram3[...] = gram_blocks(z, 2 * gram3.shape[0])


def corner_kernel(per_patch, slots, near1, near2, near3, within, gram1, gram2, gram3, z):
    fill(z, slots, per_patch, ((1, 1, within, 0), (1, -1, within, per_patch)))
    more1, more2, more3 = gram_blocks(z, 2 * near3.shape[0])
    gram1[...] = near1[...] + more1
    gram2[...] = near2[...] + more2
    gram3[...] = near3[...] + more3


def weight_kernel(per_patch, slots, near1, near2, near3, across, out, z):
    half = near3.shape[0]
    total = 2 * half
    tiles = (
        (-1, 1, across, 0),
        (-1, -1, across, per_patch),
    )
    fill(z, slots, per_patch, tiles)
    gram1, gram2, gram3 = gram_blocks(z, total)
    gram1, gram2 = gram1 + near1[...], gram2 + near2[...]
    drive = jnp.concatenate([gram1[half:], gram2[half:]], axis=1)
    s11 = gram1[:half] + eye(half)
    s12 = gram2[:half]
    s22 = gram3 + near3[...] + eye(half)
    inv11 = spd_inverse(s11)
    w = jnp.dot(inv11, s12, precision=HI)
    schur = s22 - lax.dot_general(s12, w, (((0,), (0,)), ((), ())), precision=HI)
    inv22 = spd_inverse(0.5 * (schur + schur.T))
    low = jnp.dot(w, inv22, precision=HI)
    inv = jnp.concatenate(
        [
            jnp.concatenate([inv11 + lax.dot_general(low, w, NT, precision=HI), -low], axis=1),
            jnp.concatenate([-low.T, inv22], axis=1),
        ],
        axis=0,
    )
    out[...] = 0.5 * inv + full(drive, inv)[0:1]


def update_kernel(weight, state, out):
    parts, rows, members, cols = state.shape
    x = patch_matrix(state)
    mean = jnp.sum(x, axis=0, keepdims=True) * (1.0 / (parts * members))
    anomaly = x - mean
    result = product3(weight[...], anomaly) + (mean + 0.5 * anomaly)
    for p in range(parts):
        for i in range(rows):
            out[p, i] = result[p * members : (p + 1) * members, i * cols : (i + 1) * cols]


def output_kernel(state, out, near, done):
    blocks, rows, members, cols = state.shape
    step = members // done.shape[0]
    copies = []
    for g in range(done.shape[0]):
        at = pl.ds(g * step, step)
        for b in range(blocks):
            for i in range(rows):
                near[at, i, b * cols : (b + 1) * cols] = state[b, i, at]
        copies.append(pltpu.make_async_copy(near.at[at], out.at[at], done.at[g]))
        copies[-1].start()
    for copy in copies:
        copy.wait()


VMEM = pl.BlockSpec(memory_space=pltpu.VMEM)
HBM = pl.BlockSpec(memory_space=pltpu.HBM)
SMEM = pl.BlockSpec(memory_space=pltpu.SMEM)
PARAMS = pltpu.CompilerParams(vmem_limit_bytes=20 * 1024 * 1024)


def f32(*shape):
    return jax.ShapeDtypeStruct(shape, jnp.float32)


def paired(x, axis, first):
    n = lax.axis_size(axis)
    pairs = [(i, (i + 1) % n) for i in range(first, n, 2)]
    return lax.ppermute(x, axis, pairs + [(j, i) for i, j in pairs])


def swap(x):
    return lax.all_to_all(x, "member", split_axis=0, concat_axis=0, tiled=True)


def on_device(ensemble, speed_row, speed_col, obs_cell, obs_value, obs_var, obs_count, loc_slots):
    members, rows, width = ensemble.shape
    parts = lax.axis_size("member")
    cols = width // parts
    groups = members // SUB
    per_patch, obs = obs_cell.shape[3:]
    total = parts * members

    planes = ensemble.transpose(1, 0, 2)
    own_cell = obs_cell[0, 0, 0]
    across, within, cells = pl.pallas_call(
        edge_kernel,
        out_shape=(
            f32(2 * groups + 1, SUB, width),
            f32(2 * groups + 1, SUB, width),
            jax.ShapeDtypeStruct((parts, per_patch, obs), jnp.int32),
        ),
        in_specs=[HBM] * 4,
        out_specs=(VMEM, VMEM, VMEM),
        scratch_shapes=[
            pltpu.VMEM(ensemble.shape, jnp.float32),
            pltpu.VMEM(speed_row.shape, jnp.float32),
            pltpu.VMEM(speed_col.shape, jnp.float32),
            pltpu.VMEM((per_patch, obs), jnp.int32),
            pltpu.SemaphoreType.DMA((groups + 3,)),
        ],
        compiler_params=pltpu.CompilerParams(vmem_limit_bytes=62 * 1024 * 1024),
        name="edges",
    )(ensemble, speed_row, speed_col, own_cell)
    across = paired(across, "space", 1)
    within = paired(within, "space", 0)
    fresh, state = pl.pallas_call(
        advect_kernel,
        out_shape=(f32(parts, rows, members, cols), f32(parts, rows, members, cols)),
        in_specs=[VMEM] * 5,
        out_specs=(VMEM, HBM),
        scratch_shapes=[
            pltpu.VMEM((rows + 2, 4, SUB, width), jnp.float32),
            pltpu.SemaphoreType.DMA((groups,)),
        ],
        compiler_params=PARAMS,
        name="advect",
    )(planes, across, within, speed_row, speed_col)
    cell = swap(cells)
    raw = pl.pallas_call(
        gather_kernel,
        out_shape=f32(parts, per_patch, members, obs),
        in_specs=[VMEM] * 2,
        out_specs=VMEM,
        compiler_params=PARAMS,
        name="gather",
    )(fresh, cell)
    raw = swap(raw)
    tiles = pl.pallas_call(
        tile_kernel,
        out_shape=f32(per_patch, total + SUB, obs),
        in_specs=[SMEM] + [VMEM] * 3,
        out_specs=VMEM,
        compiler_params=PARAMS,
        name="tiles",
    )(obs_count[0, 0, 0], raw, obs_value[0, 0, 0], obs_var[0, 0, 0])
    within = paired(tiles, "space", 0)
    across = paired(tiles, "space", 1)
    even_z = paired(tiles, "member", 0)
    odd_z = paired(tiles, "member", 1)
    both_z = jnp.concatenate([even_z, odd_z])
    state = swap(state)
    late_z, across, within = lax.optimization_barrier((both_z, across, within))
    within_c = paired(late_z, "space", 0)
    across_c = paired(both_z, "space", 1)
    slots = loc_slots[0, 0, 0]
    half = total // 2
    depth = per_patch * obs
    near = pl.pallas_call(
        functools.partial(near_kernel, per_patch),
        out_shape=(f32(half + SUB, half), f32(half + SUB, half), f32(half, half)),
        in_specs=[SMEM] + [VMEM] * 5,
        out_specs=(VMEM, VMEM, VMEM),
        scratch_shapes=[pltpu.VMEM((total + SUB, 5 * depth), jnp.float32)],
        compiler_params=PARAMS,
        cost_estimate=pl.CostEstimate(
            flops=240 * total * total * depth, bytes_accessed=12 * (total + SUB) * depth * 4, transcendentals=0
        ),
        name="near_gram",
    )(slots, tiles, odd_z, even_z, across, within)
    near = pl.pallas_call(
        functools.partial(corner_kernel, per_patch),
        out_shape=(f32(half + SUB, half), f32(half + SUB, half), f32(half, half)),
        in_specs=[SMEM] + [VMEM] * 4,
        out_specs=(VMEM, VMEM, VMEM),
        scratch_shapes=[pltpu.VMEM((total + SUB, 2 * depth), jnp.float32)],
        compiler_params=PARAMS,
        cost_estimate=pl.CostEstimate(
            flops=6 * total * total * depth, bytes_accessed=12 * total * total, transcendentals=0
        ),
        name="corner_gram",
    )(slots, *near, within_c)
    weight = pl.pallas_call(
        functools.partial(weight_kernel, per_patch),
        out_shape=f32(total, total),
        in_specs=[SMEM] + [VMEM] * 4,
        out_specs=VMEM,
        scratch_shapes=[pltpu.VMEM((total + SUB, 2 * depth), jnp.float32)],
        compiler_params=PARAMS,
        cost_estimate=pl.CostEstimate(
            flops=120 * total * total * depth, bytes_accessed=12 * total * total, transcendentals=0
        ),
        name="weights",
    )(slots, *near, across_c)
    state = pl.pallas_call(
        update_kernel,
        out_shape=f32(parts, rows, members, cols),
        in_specs=[VMEM] * 2,
        out_specs=VMEM,
        compiler_params=PARAMS,
        name="update",
    )(weight, state)
    state = swap(state)
    return pl.pallas_call(
        output_kernel,
        out_shape=f32(members, rows, width),
        in_specs=[VMEM],
        out_specs=HBM,
        scratch_shapes=[
            pltpu.VMEM((members, rows, width), jnp.float32),
            pltpu.SemaphoreType.DMA((4,)),
        ],
        compiler_params=PARAMS,
        name="output",
    )(state)


def solution(mesh):
    return jax.shard_map(
        on_device,
        mesh=mesh,
        in_specs=(
            P("member", "space", None),
            P("space", None),
            P("space", None),
            P("space", "member", None, None, None),
            P("space", "member", None, None, None),
            P("space", "member", None, None, None),
            P("space", "member", None, None),
            P("space", "member", None, None),
        ),
        out_specs=P("member", "space", None),
        check_vma=False,
    )
```
